128 devices in a mesh: expert: 32 (over y, x, z_lo), slab: 4 (over z_hi, core).
Axes of the slice: x: 4, y: 4, z: 4 (z_hi: 2, z_lo: 2; z = z_hi * 2 + z_lo), core: 2. Of those that a mesh axis runs over, the one named last changes fastest.
Arguments:
- tokens: bfloat16 [8192, 4096], P('expert', 'slab'), may hold values from -45 to 45
- grad_out: bfloat16 [8192, 4096], P('expert', 'slab'), may hold values from -3 to 3
- position: int32 [8192], P('expert'), may hold values from 0 to 8191, as said below
- centroid: bfloat16 [32, 4096], P('expert'), may hold values from -0.09375 to 0.09375
- gain: bfloat16 [32, 4096], P('expert'), may hold values from 0.099609375 to 1.8984375
- w_in: bfloat16 [32, 4096, 4096], P('expert', None, 'slab'), may hold values from -0.09375 to 0.09375
- w_out: bfloat16 [32, 4096, 4096], P('expert', 'slab'), may hold values from -0.09375 to 0.09375
Outputs:
- input_grad: bfloat16 [8192, 4096], P('expert', 'slab')
- centroid_grad: float32 [32, 4096], P('expert', 'slab')
The draws below stay inside these ranges and needn't reach their ends.
Inputs may be any that keep to these rules, and one draw needn't show every extreme that they name: position is a permutation of the token numbers, so every expert gets exactly 256 tokens; the 256 tokens of one index of expert go at most 12 to one expert, and in every draw some index sends exactly 12 to some expert.
All inputs are finite; a program needn't handle non-finite values.
Results may differ from the reference program's by a relative error of at most 0.015.
Values may be sent and summed in bfloat16 or wider, within the bound.
A program may use at most 128 MiB of HBM per device.

```python
import math
import jax
import jax.numpy as jnp
from jax import lax

D = 4096
FF = 4096
TOK_DEV = 256
EXPERTS = 32
TOKENS = 8192
N_SLAB = 4


def draw_tokens(key, part):
    key = jax.random.fold_in(key, 5)
    key_base, key_rows, key_cols = jax.random.split(key, 3)
    base = jax.random.normal(key_base, (TOKENS, D))
    base = jnp.clip(base, -5.0, 5.0)
    row_scale = jnp.exp(jax.random.uniform(key_rows, (TOKENS, 1), minval=math.log(0.3), maxval=math.log(3.0)))
    col_scale = jnp.exp(jax.random.uniform(key_cols, (1, D), minval=math.log(0.3), maxval=math.log(3.0)))
    return (base * row_scale * col_scale).astype(jnp.bfloat16)


def draw_position(key, part):
    key = jax.random.fold_in(key, 11)
    key_label, key_shift, key_order = jax.random.split(key, 3)
    mean_load = TOK_DEV // EXPERTS
    high_step = mean_load // 2
    low_step = mean_load // 4
    relabel = jax.random.permutation(key_label, EXPERTS)
    shifts = jax.random.permutation(key_shift, EXPERTS)[:4]
    source = jnp.arange(EXPERTS, dtype=jnp.int32)[:, None]
    column = jnp.arange(EXPERTS, dtype=jnp.int32)[None, :]

    def bump(shift):
        return (column == (source + shift) % EXPERTS).astype(jnp.int32)
    loads = mean_load + high_step * (bump(shifts[0]) - bump(shifts[1])) + low_step * (bump(shifts[2]) - bump(shifts[3]))
    counts = jnp.zeros((EXPERTS, EXPERTS), jnp.int32).at[:, relabel].set(loads)
    column_start = jnp.cumsum(counts, axis=0) - counts
    row_cum = jnp.cumsum(counts, axis=1)
    slot_index = jnp.arange(TOK_DEV, dtype=jnp.int32)
    sorted_expert = jnp.sum((row_cum[:, None, :] <= slot_index[None, :, None]).astype(jnp.int32), axis=2)
    row_start = jnp.take_along_axis(row_cum - counts, sorted_expert, axis=1)
    rank_in = slot_index[None, :] - row_start
    value = sorted_expert * TOK_DEV + jnp.take_along_axis(column_start, sorted_expert, axis=1) + rank_in
    orders = jax.vmap(lambda sub_key: jax.random.permutation(sub_key, TOK_DEV))(jax.random.split(key_order, EXPERTS))
    result = jnp.zeros((EXPERTS, TOK_DEV), jnp.int32).at[source, orders].set(value)
    return result.reshape(TOKENS)


def steps_of(own_key, dims, cuts, smallest, top_value):
    level = 1.0
    for dim, blocks in cuts:
        heights = jax.random.uniform(jax.random.fold_in(jax.random.fold_in(own_key, 6), dim), (blocks,), jnp.float32, smallest / len(cuts), top_value / len(cuts))
        level = level * jnp.repeat(jnp.exp(heights), dims[dim] // blocks).reshape((-1,) + (1,) * (len(dims) - 1 - dim))
    return level


def bell_draw(own_key, extent, width, most, cuts=(), kind=jnp.bfloat16):
    drawn = jax.random.normal(own_key, extent, jnp.float32) * width
    if len(cuts) > 0:
        drawn = steps_of(own_key, extent, cuts, -0.22, 0.18) * drawn
    return jnp.clip(drawn, min=-most, max=most).astype(kind)


def setup_inputs(seed: int = 0) -> dict:
    key_list = jax.random.split(jax.random.key(seed), 8)
    return {
        "tokens": draw_tokens(jax.random.fold_in(key_list[7], 71), 0),
        "grad_out": bell_draw(key_list[1], (TOKENS, D), 0.5, 3.0, ((0, 32), (1, 4))),
        "position": draw_position(jax.random.fold_in(key_list[7], 71), 0),
        "centroid": bell_draw(key_list[3], (EXPERTS, D), D ** -0.5, 0.09375, ((0, 32),)),
        "gain": jnp.clip(1.0 + 0.18 * jax.random.normal(key_list[4], (EXPERTS, D), jnp.float32), 0.099609375, 1.8984375).astype(jnp.bfloat16),
        "w_in": bell_draw(key_list[5], (EXPERTS, D, FF), D ** -0.5, 0.09375, ((0, 32), (2, 4))),
        "w_out": bell_draw(key_list[6], (EXPERTS, FF, D), FF ** -0.5, 0.09375, ((0, 32), (1, 4))),
    }


gelu_root = math.sqrt(2.0 / math.pi)

def gelu_pair(pre):
    tangent = jnp.tanh(gelu_root * (pre + 0.044715 * pre * pre * pre))
    value = 0.5 * pre * (1.0 + tangent)
    slope = 0.5 * (1.0 + tangent) + 0.5 * pre * (1.0 - tangent * tangent) * gelu_root * (1.0 + 3.0 * 0.044715 * pre * pre)
    return (value, slope)

def expert_grad(bundle):
    rows_x, rows_dy, center, gain_row, weight_in, weight_out = bundle
    logit = jnp.dot(rows_x, center, preferred_element_type=jnp.float32)
    gate = jax.nn.sigmoid(logit)
    wide_x = rows_x.astype(jnp.float32)
    row_mean = lax.optimization_barrier(jnp.mean(wide_x, axis=1))
    centered = wide_x - row_mean[:, None]
    variance = lax.optimization_barrier(jnp.mean(centered * centered, axis=1))
    inv_scale = lax.rsqrt(variance + 1e-05)
    hat = centered * inv_scale[:, None]
    gain_wide = gain_row.astype(jnp.float32)
    normed = (hat * gain_wide[None, :]).astype(jnp.bfloat16)
    pre = jnp.dot(normed, weight_in, preferred_element_type=jnp.float32)
    active, slope = gelu_pair(pre)
    back = jnp.dot(rows_dy, weight_out.T, preferred_element_type=jnp.float32)
    gate_total = lax.optimization_barrier(jnp.sum(active * back, axis=1))
    delta = (gate[:, None] * back * slope).astype(jnp.bfloat16)
    block = FF // N_SLAB
    delta_blocks = delta.astype(jnp.float32).reshape(delta.shape[0], N_SLAB, block)
    weight_blocks = weight_in.astype(jnp.float32).reshape(D, N_SLAB, block)
    partial_value = jnp.einsum('rsf,dsf->srd', delta_blocks, weight_blocks).astype(jnp.bfloat16)
    grad_normed = lax.optimization_barrier(jnp.sum(partial_value.astype(jnp.float32), axis=0))
    scaled = grad_normed * gain_wide[None, :]
    mean_one = lax.optimization_barrier(jnp.mean(scaled, axis=1))
    mean_two = lax.optimization_barrier(jnp.mean(scaled * hat, axis=1))
    gate_grad = gate_total * gate * (1.0 - gate)
    grad_rows = inv_scale[:, None] * (scaled - mean_one[:, None] - hat * mean_two[:, None])
    grad_rows = (grad_rows + gate_grad[:, None] * center.astype(jnp.float32)[None, :]).astype(jnp.bfloat16)
    center_grad = lax.optimization_barrier(jnp.sum(wide_x * gate_grad[:, None], axis=0))
    return (grad_rows, center_grad)

def reference(tokens, grad_out, position, centroid, gain, w_in, w_out):
    token_at = jnp.zeros((TOKENS,), jnp.int32).at[position].set(jnp.arange(TOKENS, dtype=jnp.int32))
    sorted_x = jnp.take(tokens, token_at, axis=0).reshape(EXPERTS, TOK_DEV, D)
    sorted_dy = jnp.take(grad_out, token_at, axis=0).reshape(EXPERTS, TOK_DEV, D)
    grads, center_grads = lax.map(expert_grad, (sorted_x, sorted_dy, centroid, gain, w_in, w_out))
    input_grad = jnp.take(grads.reshape(TOKENS, D), position, axis=0)
    return (input_grad, center_grads)
```

```python
import functools
import math

import jax
import jax.numpy as jnp
from jax import lax
from jax.experimental import pallas as pl
from jax.experimental.pallas import tpu as pltpu
from jax.sharding import PartitionSpec as P

F32 = jnp.float32
BF16 = jnp.bfloat16
MESH = pl.DeviceIdType.MESH
ROWS = 16
ROOT = math.sqrt(2.0 / math.pi)
N_SLAB = 4


def iota(shape, dim):
    return lax.broadcasted_iota(jnp.int32, shape, dim)


def onehot(mask):
    return jnp.where(mask, 1.0, 0.0).astype(BF16)


def dot(a, b):
    return jnp.dot(a, b, preferred_element_type=F32)


def dot_t(a, b):
    return lax.dot_general(a, b, (((1,), (1,)), ((), ())), preferred_element_type=F32)


def kernel(
    n_exp,
    pos_ref,
    cent_ref,
    gain_ref,
    tok_hbm,
    dy_hbm,
    win_hbm,
    wout_hbm,
    out_ref,
    cgrad_ref,
    tok,
    gdy,
    win,
    wout,
    pick,
    pick_t,
    px,
    pd,
    rx,
    rd,
    comp,
    comp_t,
    xf,
    df,
    nx,
    pre,
    act,
    slp,
    bk,
    delta,
    usum,
    cols,
    stat,
    part_send,
    part_recv,
    far_acc,
    far_send,
    far_recv,
    mine_send,
    mine_recv,
    own,
    yy,
    pg,
    rg,
    lsem,
    a2a_s,
    a2a_r,
    ag_s,
    ag_r,
    rs_s,
    rs_r,
    st_s,
    st_r,
):
    rows, width = tok.shape
    full = N_SLAB * width
    ff = win.shape[1]
    quarter = width // 4
    slots = n_exp * ROWS
    me = lax.axis_index("expert")
    slab = lax.axis_index("slab")
    hi, core = slab // 2, slab % 2
    partner = hi * 2 + (1 - core)
    far = (1 - hi) * 2 + core
    far_partner = (1 - hi) * 2 + (1 - core)

    cp_tok = pltpu.make_async_copy(tok_hbm, tok, lsem.at[0])
    cp_dy = pltpu.make_async_copy(dy_hbm, gdy, lsem.at[1])
    cp_win = pltpu.make_async_copy(win_hbm, win, lsem.at[2])
    cp_wout = pltpu.make_async_copy(wout_hbm, wout, lsem.at[3])
    cp_tok.start()
    cp_dy.start()

    bar = pltpu.get_barrier_semaphore()

    @pl.loop(1, n_exp)
    def _(k):
        pl.semaphore_signal(
            bar, inc=1, device_id={"expert": lax.rem(me + k, n_exp)}, device_id_type=MESH
        )

    for peer in (partner, far, far_partner):
        pl.semaphore_signal(bar, inc=1, device_id={"slab": peer}, device_id_type=MESH)
    cp_win.start()
    cp_wout.start()

    pos = pos_ref[...]
    tgt = lax.div(pos, rows)
    row = pos - tgt * rows
    hit = iota((n_exp, rows), 0) == tgt
    before = dot(onehot(hit), onehot(iota((rows, rows), 0) < iota((rows, rows), 1)))
    rank = jnp.sum(jnp.where(hit, before, 0.0), axis=0, keepdims=True).astype(jnp.int32)
    third = lax.shift_right_logical(rank * 11, 5)
    rem3 = rank - 3 * third
    slot = [tgt * ROWS + rank]
    for j in range(3):
        slot.append(jnp.where(rem3 == j, tgt * ROWS + 12 + third, -1))
    for k in range(4):
        pick[k] = onehot(iota((slots, rows), 0) == slot[k])

    row_one = jnp.broadcast_to((row + 1).astype(F32), (128, rows))
    meta = None
    for k in range(4):
        marks = jnp.where(iota((128, rows), 0) // 32 == k, row_one, 0.0).astype(BF16)
        term = dot_t(pick[k], marks)
        meta = term if meta is None else meta + term
    px[:, pl.ds(3 * quarter, 128)] = meta.astype(BF16)

    def pack(into, take, source):
        for j in range(3):
            cols_j = pl.ds(j * quarter, quarter)
            value = dot(take[0], source[:, cols_j]) + dot(
                take[1 + j], source[:, pl.ds(3 * quarter, quarter)]
            )
            into[:, cols_j] = value.astype(BF16)

    mine = pl.ds(pl.multiple_of(me * ROWS, ROWS), ROWS)

    def send_all(source, target, idx):
        @pl.loop(1, n_exp)
        def _(k):
            d = lax.rem(me + k, n_exp)
            pltpu.make_async_remote_copy(
                src_ref=source.at[pl.ds(pl.multiple_of(d * ROWS, ROWS), ROWS)],
                dst_ref=target.at[mine],
                send_sem=a2a_s.at[idx],
                recv_sem=a2a_r.at[idx],
                device_id={"expert": d},
                device_id_type=MESH,
            ).start()

    def wait_bytes(ref, sem):
        part = ref.at[pl.ds(0, (n_exp - 1) * ROWS)]
        pltpu.make_async_copy(part, part, sem).wait()

    cp_tok.wait()
    pack(px, pick, tok)
    rx[mine, :] = px[mine, :]
    pl.semaphore_wait(bar, n_exp - 1 + 3)
    send_all(px, rx, 0)
    cp_dy.wait()
    pack(pd, pick, gdy)
    rd[mine, :] = pd[mine, :]
    send_all(pd, rd, 1)

    turned = [
        jnp.transpose(jnp.broadcast_to(slot[k].astype(F32), (128, rows)))[:, 0:1] for k in range(4)
    ]
    for k in range(4):
        pick_t[k] = onehot(iota((rows, slots), 1).astype(F32) == turned[k])
    cp_win.wait()
    gain_rows = jnp.broadcast_to(gain_ref[...], (16, full))

    @pl.loop(0, ff // 256)
    def _(n):
        cs = pl.ds(pl.multiple_of(n * 256, 256), 256)
        usum[:, cs] = dot(gain_rows, win[:, cs])[0:8]

    def gather_copy(buf, which, tile, source, kind, to):
        cs = pl.ds(tile * quarter, quarter)
        idx = (which * 3 + kind) * 4 + tile
        return pltpu.make_async_remote_copy(
            src_ref=buf.at[source, :, cs],
            dst_ref=buf.at[source, :, cs],
            send_sem=ag_s.at[idx],
            recv_sem=ag_r.at[idx],
            device_id={"slab": to},
            device_id_type=MESH,
        )

    def dense(recv, buf, which):
        for tile in range(4):
            cs = pl.ds(tile * quarter, quarter)
            if tile < 3:
                value = dot(comp[0], recv[:, cs])
            else:
                value = dot(comp[1], recv[:, pl.ds(0, quarter)])
                value += dot(comp[2], recv[:, pl.ds(quarter, quarter)])
                value += dot(comp[3], recv[:, pl.ds(2 * quarter, quarter)])
            buf[slab, :, cs] = value.astype(BF16)
            gather_copy(buf, which, tile, slab, 0, far).start()
            gather_copy(buf, which, tile, slab, 1, partner).start()

    def forward(buf, which, tile):
        gather_copy(buf, which, tile, far, 0, far).wait_recv()
        gather_copy(buf, which, tile, far, 2, partner).start()

    wait_bytes(rx, a2a_r.at[0])
    marks_in = rx[:, pl.ds(3 * quarter, 128)].astype(F32)
    marks_t = jnp.transpose(marks_in)
    for k in range(4):
        comp[k] = onehot((iota((rows, slots), 0) + 1).astype(F32) == marks_t[32 * k : 32 * k + 1])
    dense(rx, xf, 0)
    for k in range(4):
        comp_t[k] = onehot(
            (iota((slots, rows), 1) + 1).astype(F32) == marks_in[:, 32 * k : 32 * k + 1]
        )
    wait_bytes(rd, a2a_r.at[1])
    dense(rd, df, 1)

    for tile in range(4):
        forward(xf, 0, tile)
    for tile in range(4):
        gather_copy(xf, 0, tile, partner, 1, partner).wait_recv()
    for tile in range(4):
        gather_copy(xf, 0, tile, far_partner, 2, partner).wait_recv()

    step = 16

    @pl.loop(0, rows // step)
    def _(i):
        rs = pl.ds(pl.multiple_of(i * step, step), step)
        xs = [xf[b, rs, :].astype(F32) for b in range(N_SLAB)]
        total = None
        logit = None
        for b in range(N_SLAB):
            c_b = cent_ref[:, pl.ds(b * width, width)].astype(F32)
            t_b = jnp.sum(xs[b], axis=1, keepdims=True)
            l_b = jnp.sum(xs[b] * c_b, axis=1, keepdims=True)
            total = t_b if total is None else total + t_b
            logit = l_b if logit is None else logit + l_b
        mean = total * (1.0 / full)
        spread = None
        for b in range(N_SLAB):
            xs[b] = xs[b] - mean
            v_b = jnp.sum(xs[b] * xs[b], axis=1, keepdims=True)
            spread = v_b if spread is None else spread + v_b
        inv = lax.rsqrt(spread * (1.0 / full) + 1e-05)
        for b in range(N_SLAB):
            g_b = gain_ref[:, pl.ds(b * width, width)].astype(F32)
            nx[b, rs, :] = (xs[b] * inv * g_b).astype(BF16)
        gate = 1.0 / (1.0 + jnp.exp(-logit))
        cols[0, rs, :] = jnp.broadcast_to(mean, (step, 128))
        cols[1, rs, :] = jnp.broadcast_to(inv, (step, 128))
        cols[2, rs, :] = jnp.broadcast_to(gate, (step, 128))

    @pl.loop(0, ff // 256)
    def _(n):
        cs = pl.ds(pl.multiple_of(n * 256, 256), 256)
        acc = dot(nx[0], win[pl.ds(0, width), cs])
        for b in range(1, N_SLAB):
            acc += dot(nx[b], win[pl.ds(b * width, width), cs])
        pre[:, cs] = acc

    @pl.loop(0, rows // step)
    def _(i):
        rs = pl.ds(pl.multiple_of(i * step, step), step)
        p = pre[rs, :]
        gate = cols[2, rs, 0:1]
        sq = p * p
        tangent = jnp.tanh(ROOT * (p + 0.044715 * p * sq))
        half = 0.5 * (1.0 + tangent)
        act[rs, :] = p * half
        slp[rs, :] = gate * (
            half + 0.5 * p * (1.0 - tangent * tangent) * ROOT * (1.0 + 3.0 * 0.044715 * sq)
        )

    def back_from(b, first):
        base = pl.multiple_of(b * width, width)

        @pl.loop(0, ff // 256)
        def _(n):
            rs = pl.ds(pl.multiple_of(n * 256, 256), 256)
            value = dot_t(df[b], wout[rs, pl.ds(base, width)])
            if first:
                bk[:, rs] = value
            else:
                bk[:, rs] += value

    cp_wout.wait()
    back_from(slab, True)
    for tile in range(4):
        gather_copy(df, 1, tile, partner, 1, partner).wait_recv()
    back_from(partner, False)
    for tile in range(4):
        forward(df, 1, tile)
    back_from(far, False)
    for tile in range(4):
        gather_copy(df, 1, tile, far_partner, 2, partner).wait_recv()
    back_from(far_partner, False)

    @pl.loop(0, rows // step)
    def _(i):
        rs = pl.ds(pl.multiple_of(i * step, step), step)
        b = bk[rs, :]
        d = (b * slp[rs, :]).astype(BF16)
        delta[rs, :] = d
        d = d.astype(F32)
        g_sum = jnp.sum(act[rs, :] * b, axis=1, keepdims=True)
        one = jnp.sum(d * usum[0:1, :], axis=1, keepdims=True)
        two = jnp.sum(d * pre[rs, :], axis=1, keepdims=True)
        lane = iota((step, 128), 1)
        cols[3, rs, :] = jnp.where(lane == 0, g_sum, jnp.where(lane == 1, one, two))

    def grad_tile(b, tile):
        base = pl.multiple_of(b * width + tile * quarter, quarter)
        return dot_t(delta[...], win[pl.ds(base, quarter), :])

    def reduce_copy(kind, tile, src, dst, to):
        return pltpu.make_async_remote_copy(
            src_ref=src.at[tile],
            dst_ref=dst.at[tile],
            send_sem=rs_s.at[kind * 4 + tile],
            recv_sem=rs_r.at[kind * 4 + tile],
            device_id={"slab": to},
            device_id_type=MESH,
        )

    for tile in range(4):
        part_send[tile] = grad_tile(far_partner, tile).astype(BF16)
        reduce_copy(0, tile, part_send, part_recv, partner).start()
    for tile in range(4):
        far_acc[...] = grad_tile(far, tile)
        reduce_copy(0, tile, part_send, part_recv, partner).wait_recv()
        far_send[tile] = (far_acc[...] + part_recv[tile].astype(F32)).astype(BF16)
        reduce_copy(1, tile, far_send, far_recv, far).start()

    def stat_copy(n, to):
        return pltpu.make_async_remote_copy(
            src_ref=stat.at[0],
            dst_ref=stat.at[n],
            send_sem=st_s.at[n],
            recv_sem=st_r.at[n],
            device_id={"slab": to},
            device_id_type=MESH,
        )

    stat[0] = jnp.transpose(cols[3])[0:8]
    peers = ((1, partner), (2, far), (3, far_partner))
    for n, to in peers:
        stat_copy(n, to).start()
    for tile in range(4):
        mine_send[tile] = grad_tile(partner, tile).astype(BF16)
        reduce_copy(2, tile, mine_send, mine_recv, partner).start()
    for tile in range(4):
        own[tile] = grad_tile(slab, tile)
    for n, to in peers:
        stat_copy(n, to).wait_recv()
    sums = stat[0] + stat[1] + stat[2] + stat[3]
    sums = jnp.transpose(jnp.concatenate([sums] * 16, axis=0))
    gate = cols[2, :, 0:1]
    gate_grad = sums[:, 0:1] * gate * (1.0 - gate)
    mean_one = sums[:, 1:2] * (1.0 / full)
    mean_two = sums[:, 2:3] * (1.0 / full)
    mean = cols[0, :, 0:1]
    inv = cols[1, :, 0:1]
    for tile in range(4):
        cs = pl.ds(tile * quarter, quarter)
        glob = pl.ds(pl.multiple_of(slab * width + tile * quarter, quarter), quarter)
        x = xf[slab, :, cs].astype(F32)
        cgrad_ref[:, cs] = jnp.sum(x * gate_grad, axis=0, keepdims=True)
        reduce_copy(2, tile, mine_send, mine_recv, partner).wait_recv()
        total = own[tile] + mine_recv[tile].astype(F32)
        reduce_copy(1, tile, far_send, far_recv, far).wait_recv()
        total = total + far_recv[tile].astype(F32)
        scaled = total * gain_ref[:, glob].astype(F32)
        hat = (x - mean) * inv
        value = inv * (scaled - mean_one - hat * mean_two)
        value = value + gate_grad * cent_ref[:, glob].astype(F32)
        yy[:, cs] = value.astype(BF16)

    pack(pg, comp_t, yy)
    rg[mine, :] = pg[mine, :]
    send_all(pg, rg, 2)
    wait_bytes(rg, a2a_r.at[2])
    for tile in range(3):
        cs = pl.ds(tile * quarter, quarter)
        out_ref[:, cs] = dot(pick_t[0], rg[:, cs]).astype(BF16)
    value = dot(pick_t[1], rg[:, pl.ds(0, quarter)])
    value += dot(pick_t[2], rg[:, pl.ds(quarter, quarter)])
    value += dot(pick_t[3], rg[:, pl.ds(2 * quarter, quarter)])
    out_ref[:, pl.ds(3 * quarter, quarter)] = value.astype(BF16)

    wait_bytes(px, a2a_s.at[0])
    wait_bytes(pd, a2a_s.at[1])
    wait_bytes(pg, a2a_s.at[2])
    for tile in range(4):
        for which, buf in ((0, xf), (1, df)):
            gather_copy(buf, which, tile, slab, 0, far).wait_send()
            gather_copy(buf, which, tile, slab, 1, partner).wait_send()
            gather_copy(buf, which, tile, far, 2, partner).wait_send()
        reduce_copy(0, tile, part_send, part_recv, partner).wait_send()
        reduce_copy(1, tile, far_send, far_recv, far).wait_send()
        reduce_copy(2, tile, mine_send, mine_recv, partner).wait_send()
    for n, to in peers:
        stat_copy(n, to).wait_send()


def per_device(tokens, grad_out, position, centroid, gain, w_in, w_out):
    n_exp = lax.axis_size("expert")
    rows, width = tokens.shape
    full = centroid.shape[1]
    ff = w_in.shape[2]
    slots = n_exp * ROWS
    quarter = width // 4
    packed = 3 * quarter
    vmem = pl.BlockSpec(memory_space=pltpu.VMEM)
    hbm = pl.BlockSpec(memory_space=pl.ANY)
    buf = pltpu.VMEM
    dma = pltpu.SemaphoreType.DMA
    return pl.pallas_call(
        functools.partial(kernel, n_exp),
        out_shape=(
            jax.ShapeDtypeStruct((rows, width), BF16),
            jax.ShapeDtypeStruct((1, width), F32),
        ),
        in_specs=[vmem, vmem, vmem, hbm, hbm, hbm, hbm],
        out_specs=(vmem, vmem),
        scratch_shapes=[
            buf((rows, width), BF16),
            buf((rows, width), BF16),
            buf((full, ff), BF16),
            buf((ff, full), BF16),
            buf((4, slots, rows), BF16),
            buf((4, rows, slots), BF16),
            buf((slots, packed + 128), BF16),
            buf((slots, packed), BF16),
            buf((slots, packed + 128), BF16),
            buf((slots, packed), BF16),
            buf((4, rows, slots), BF16),
            buf((4, slots, rows), BF16),
            buf((N_SLAB, rows, width), BF16),
            buf((N_SLAB, rows, width), BF16),
            buf((N_SLAB, rows, width), BF16),
            buf((rows, ff), F32),
            buf((rows, ff), F32),
            buf((rows, ff), F32),
            buf((rows, ff), F32),
            buf((rows, ff), BF16),
            buf((8, ff), F32),
            buf((4, rows, 128), F32),
            buf((4, 8, rows), F32),
            buf((4, rows, quarter), BF16),
            buf((4, rows, quarter), BF16),
            buf((rows, quarter), F32),
            buf((4, rows, quarter), BF16),
            buf((4, rows, quarter), BF16),
            buf((4, rows, quarter), BF16),
            buf((4, rows, quarter), BF16),
            buf((4, rows, quarter), F32),
            buf((rows, width), BF16),
            buf((slots, packed), BF16),
            buf((slots, packed), BF16),
            dma((4,)),
            dma((3,)),
            dma((3,)),
            dma((24,)),
            dma((24,)),
            dma((12,)),
            dma((12,)),
            dma((4,)),
            dma((4,)),
        ],
        compiler_params=pltpu.CompilerParams(
            collective_id=0, has_side_effects=True, vmem_limit_bytes=56 * 2**20
        ),
        cost_estimate=pl.CostEstimate(
            flops=3 * 2 * rows * full * ff, bytes_accessed=4 * full * ff, transcendentals=rows * ff
        ),
    )(position.reshape(1, rows), centroid, gain, tokens, grad_out, w_in[0], w_out[0])


def solution(mesh):
    placed = (
        P("expert", "slab"),
        P("expert", "slab"),
        P("expert"),
        P("expert", None),
        P("expert", None),
        P("expert", None, "slab"),
        P("expert", "slab", None),
    )
    return jax.shard_map(
        per_device,
        mesh=mesh,
        in_specs=placed,
        out_specs=(P("expert", "slab"), P("expert", "slab")),
        check_vma=False,
    )
```

```python
import functools
import math

import jax
import jax.numpy as jnp
from jax import lax
from jax.experimental import pallas as pl
from jax.experimental.pallas import tpu as pltpu
from jax.sharding import PartitionSpec as P

F32 = jnp.float32
BF16 = jnp.bfloat16
MESH = pl.DeviceIdType.MESH
ROWS = 16
ROOT = math.sqrt(2.0 / math.pi)
N_SLAB = 4


def iota(shape, dim):
    return lax.broadcasted_iota(jnp.int32, shape, dim)


def onehot(mask):
    return jnp.where(mask, 1.0, 0.0).astype(BF16)


def dot(a, b):
    return jnp.dot(a, b, preferred_element_type=F32)


def dot_t(a, b):
    return lax.dot_general(a, b, (((1,), (1,)), ((), ())), preferred_element_type=F32)


def kernel(
    n_exp,
    pos_ref,
    cent_ref,
    gain_ref,
    tok_hbm,
    dy_hbm,
    win_hbm,
    wout_hbm,
    out_ref,
    cgrad_ref,
    tok,
    gdy,
    win,
    wout,
    pick,
    pick_t,
    px0,
    px1,
    pd0,
    pd1,
    rx0,
    rx1,
    rd0,
    rd1,
    comp,
    comp_t,
    xf,
    df,
    nx,
    pre,
    act,
    slp,
    bk,
    delta,
    usum,
    cols,
    stat,
    part_send,
    part_recv,
    far_send,
    far_recv,
    mine_send,
    mine_recv,
    own,
    yy,
    pg0,
    pg1,
    rg0,
    rg1,
    lsem,
    a2a_s,
    a2a_r,
    ag_s,
    ag_r,
    rs_s,
    rs_r,
    st_s,
    st_r,
):
    rows, width = tok.shape
    full = N_SLAB * width
    ff = win.shape[1]
    half = width // 2
    q = half // 4
    tile_w = width // 4
    half_rows = rows // 2
    slots = n_exp * ROWS
    me = lax.axis_index("expert")
    slab = lax.axis_index("slab")
    hi, core = slab // 2, slab % 2
    partner = hi * 2 + (1 - core)
    far = (1 - hi) * 2 + core
    far_partner = (1 - hi) * 2 + (1 - core)

    cp_tok = pltpu.make_async_copy(tok_hbm, tok, lsem.at[0])
    cp_dy = pltpu.make_async_copy(dy_hbm, gdy, lsem.at[1])
    cp_win = pltpu.make_async_copy(win_hbm, win, lsem.at[2])
    cp_wout = pltpu.make_async_copy(wout_hbm, wout, lsem.at[3])
    cp_tok.start()
    cp_dy.start()

    bar = pltpu.get_barrier_semaphore()

    @pl.loop(1, n_exp)
    def _(k):
        pl.semaphore_signal(
            bar, inc=1, device_id={"expert": lax.rem(me + k, n_exp)}, device_id_type=MESH
        )

    for peer in (partner, far, far_partner):
        pl.semaphore_signal(bar, inc=1, device_id={"slab": peer}, device_id_type=MESH)
    cp_win.start()
    cp_wout.start()

    pos = pos_ref[...]
    tgt = lax.div(pos, rows)
    row = pos - tgt * rows
    hit = iota((n_exp, rows), 0) == tgt
    before = dot(onehot(hit), onehot(iota((rows, rows), 0) < iota((rows, rows), 1)))
    rank = jnp.sum(jnp.where(hit, before, 0.0), axis=0, keepdims=True).astype(jnp.int32)
    third = lax.shift_right_logical(rank * 11, 5)
    rem3 = rank - 3 * third
    slot = [tgt * ROWS + rank]
    for j in range(3):
        slot.append(jnp.where(rem3 == j, tgt * ROWS + 12 + third, -1))
    for k in range(4):
        pick[k] = onehot(iota((slots, rows), 0) == slot[k])

    row_one = jnp.broadcast_to((row + 1).astype(F32), (128, rows))
    meta = None
    for k in range(4):
        marks = jnp.where(iota((128, rows), 0) // 32 == k, row_one, 0.0).astype(BF16)
        term = dot_t(pick[k], marks)
        meta = term if meta is None else meta + term
    px0[:, pl.ds(3 * q, 128)] = meta.astype(BF16)

    mine = pl.ds(pl.multiple_of(me * ROWS, ROWS), ROWS)

    def pack(into, keep, take, source, c):
        last = source[:, pl.ds(c * half + 3 * q, q)]
        for j in range(3):
            cs = pl.ds(j * q, q)
            value = dot(take[0], source[:, pl.ds(c * half + j * q, q)]) + dot(take[1 + j], last)
            into[:, cs] = value.astype(BF16)
        keep[mine, :] = into[mine, :]

    def unpack(into, lead, take, source, c):
        into[lead + (slice(None), pl.ds(c * half, 3 * q))] = dot(
            take[0], source[:, pl.ds(0, 3 * q)]
        ).astype(BF16)
        value = dot(take[1], source[:, pl.ds(0, q)])
        value += dot(take[2], source[:, pl.ds(q, q)])
        value += dot(take[3], source[:, pl.ds(2 * q, q)])
        into[lead + (slice(None), pl.ds(c * half + 3 * q, q))] = value.astype(BF16)

    def send_all(source, target, idx):
        @pl.loop(1, n_exp)
        def _(k):
            d = lax.rem(me + k, n_exp)
            pltpu.make_async_remote_copy(
                src_ref=source.at[pl.ds(pl.multiple_of(d * ROWS, ROWS), ROWS)],
                dst_ref=target.at[mine],
                send_sem=a2a_s.at[idx],
                recv_sem=a2a_r.at[idx],
                device_id={"expert": d},
                device_id_type=MESH,
            ).start()

    def wait_bytes(ref, sem):
        part = ref.at[pl.ds(0, (n_exp - 1) * ROWS)]
        pltpu.make_async_copy(part, part, sem).wait()

    cp_tok.wait()
    pack(px0, rx0, pick, tok, 0)
    pl.semaphore_wait(bar, n_exp - 1 + 3)
    send_all(px0, rx0, 0)
    pack(px1, rx1, pick, tok, 1)
    send_all(px1, rx1, 1)
    cp_dy.wait()
    pack(pd0, rd0, pick, gdy, 0)
    pack(pd1, rd1, pick, gdy, 1)

    for k in range(4):
        turned = jnp.transpose(jnp.broadcast_to(slot[k].astype(F32), (128, rows)))[:, 0:1]
        pick_t[k] = onehot(iota((rows, slots), 1).astype(F32) == turned)
    cp_win.wait()
    gain_rows = jnp.broadcast_to(gain_ref[...], (16, full))

    @pl.loop(0, ff // 256)
    def _(n):
        cs = pl.ds(pl.multiple_of(n * 256, 256), 256)
        usum[:, cs] = dot(gain_rows, win[:, cs])[0:8]

    def gather_copy(buf, idx, rs, c, source, kind, to):
        block = buf.at[source, rs, pl.ds(c * half, half)]
        return pltpu.make_async_remote_copy(
            src_ref=block,
            dst_ref=block,
            send_sem=ag_s.at[idx * 3 + kind],
            recv_sem=ag_r.at[idx * 3 + kind],
            device_id={"slab": to},
            device_id_type=MESH,
        )

    every = pl.ds(0, rows)

    def x_copy(c, source, kind, to):
        return gather_copy(xf, c, every, c, source, kind, to)

    def d_copy(h, c, source, kind, to):
        return gather_copy(
            df, 2 + 2 * h + c, pl.ds(h * half_rows, half_rows), c, source, kind, to
        )

    def x_dense(recv, c):
        unpack(xf, (slab,), comp, recv, c)
        x_copy(c, slab, 0, far).start()
        x_copy(c, slab, 1, partner).start()

    def d_start(h, c):
        d_copy(h, c, slab, 0, far).start()
        d_copy(h, c, slab, 1, partner).start()

    wait_bytes(rx0, a2a_r.at[0])
    marks_in = rx0[:, pl.ds(3 * q, 128)].astype(F32)
    marks_t = jnp.transpose(marks_in)
    for k in range(4):
        comp[k] = onehot((iota((rows, slots), 0) + 1).astype(F32) == marks_t[32 * k : 32 * k + 1])
    x_dense(rx0, 0)
    send_all(pd0, rd0, 2)
    wait_bytes(rx1, a2a_r.at[1])
    x_dense(rx1, 1)
    send_all(pd1, rd1, 3)
    for k in range(4):
        comp_t[k] = onehot(
            (iota((slots, rows), 1) + 1).astype(F32) == marks_in[:, 32 * k : 32 * k + 1]
        )
    x_copy(0, far, 0, far).wait_recv()
    x_copy(0, far, 2, partner).start()
    wait_bytes(rd0, a2a_r.at[2])
    unpack(df, (slab,), comp, rd0, 0)
    d_start(0, 0)
    x_copy(1, far, 0, far).wait_recv()
    x_copy(1, far, 2, partner).start()
    for c in range(2):
        x_copy(c, partner, 1, partner).wait_recv()
    for c in range(2):
        x_copy(c, far_partner, 2, partner).wait_recv()

    step = 16

    @pl.loop(0, rows // step)
    def _(i):
        rs = pl.ds(pl.multiple_of(i * step, step), step)
        xs = [xf[b, rs, :].astype(F32) for b in range(N_SLAB)]
        total = None
        logit = None
        for b in range(N_SLAB):
            c_b = cent_ref[:, pl.ds(b * width, width)].astype(F32)
            t_b = jnp.sum(xs[b], axis=1, keepdims=True)
            l_b = jnp.sum(xs[b] * c_b, axis=1, keepdims=True)
            total = t_b if total is None else total + t_b
            logit = l_b if logit is None else logit + l_b
        mean = total * (1.0 / full)
        spread = None
        for b in range(N_SLAB):
            xs[b] = xs[b] - mean
            v_b = jnp.sum(xs[b] * xs[b], axis=1, keepdims=True)
            spread = v_b if spread is None else spread + v_b
        inv = lax.rsqrt(spread * (1.0 / full) + 1e-05)
        for b in range(N_SLAB):
            g_b = gain_ref[:, pl.ds(b * width, width)].astype(F32)
            nx[b, rs, :] = (xs[b] * inv * g_b).astype(BF16)
        gate = 1.0 / (1.0 + jnp.exp(-logit))
        cols[0, rs, :] = jnp.broadcast_to(mean, (step, 128))
        cols[1, rs, :] = jnp.broadcast_to(inv, (step, 128))
        cols[2, rs, :] = jnp.broadcast_to(gate, (step, 128))
    wait_bytes(rd1, a2a_r.at[3])
    unpack(df, (slab,), comp, rd1, 1)
    d_start(0, 1)
    d_start(1, 0)
    d_start(1, 1)

    for n in range(ff // 256):
        cs = pl.ds(n * 256, 256)
        acc = dot(nx[0], win[pl.ds(0, width), cs])
        for b in range(1, N_SLAB):
            acc += dot(nx[b], win[pl.ds(b * width, width), cs])
        pre[:, cs] = acc

    @pl.loop(0, rows // step, unroll=2)
    def _(i):
        rs = pl.ds(pl.multiple_of(i * step, step), step)
        p = pre[rs, :]
        gate = cols[2, rs, 0:1]
        sq = p * p
        tangent = jnp.tanh(ROOT * (p + 0.044715 * p * sq))
        mid = 0.5 * (1.0 + tangent)
        act[rs, :] = p * mid
        slp[rs, :] = gate * (
            mid + 0.5 * p * (1.0 - tangent * tangent) * ROOT * (1.0 + 3.0 * 0.044715 * sq)
        )

    cp_wout.wait()

    def back_from(h, sources, first):
        hs = pl.ds(h * half_rows, half_rows)

        for n in range(ff // 256):
            rs = pl.ds(n * 256, 256)
            value = None
            for b in sources:
                base = pl.multiple_of(b * width, width)
                term = dot_t(df[b, hs, :], wout[rs, pl.ds(base, width)])
                value = term if value is None else value + term
            if first:
                bk[hs, rs] = value
            else:
                bk[hs, rs] += value

    def grad_tile(b, tile, rs):
        base = pl.multiple_of(b * width + tile * tile_w, tile_w)
        return dot_t(delta[rs, :], win[pl.ds(base, tile_w), :])

    def reduce_copy(kind, n, src, dst, to):
        return pltpu.make_async_remote_copy(
            src_ref=src.at[n],
            dst_ref=dst.at[n],
            send_sem=rs_s.at[kind * 8 + n],
            recv_sem=rs_r.at[kind * 8 + n],
            device_id={"slab": to},
            device_id_type=MESH,
        )

    def part_copy(n):
        return reduce_copy(0, n, part_send, part_recv, partner)

    def far_copy(n):
        return reduce_copy(1, n, far_send, far_recv, far)

    def mine_copy(n):
        return reduce_copy(2, n, mine_send, mine_recv, partner)

    for h in range(2):
        hs = pl.ds(h * half_rows, half_rows)
        for c in range(2):
            d_copy(h, c, partner, 1, partner).wait_recv()
        back_from(h, (slab, partner), True)
        for c in range(2):
            d_copy(h, c, far, 0, far).wait_recv()
            d_copy(h, c, far, 2, partner).start()
        back_from(h, (far,), False)
        for c in range(2):
            d_copy(h, c, far_partner, 2, partner).wait_recv()
        back_from(h, (far_partner,), False)

        @pl.loop(0, half_rows // step, unroll=4)
        def _(i):
            rs = pl.ds(pl.multiple_of(h * half_rows + i * step, step), step)
            b = bk[rs, :]
            d = (b * slp[rs, :]).astype(BF16)
            delta[rs, :] = d
            d = d.astype(F32)
            g_sum = jnp.sum(act[rs, :] * b, axis=1, keepdims=True)
            one = jnp.sum(d * usum[0:1, :], axis=1, keepdims=True)
            two = jnp.sum(d * pre[rs, :], axis=1, keepdims=True)
            lane = iota((step, 128), 1)
            cols[3, rs, :] = jnp.where(lane == 0, g_sum, jnp.where(lane == 1, one, two))

        for tile in range(4):
            part_send[h * 4 + tile] = grad_tile(far_partner, tile, hs).astype(BF16)
            part_copy(h * 4 + tile).start()
        for tile in range(4):
            value = grad_tile(far, tile, hs)
            part_copy(h * 4 + tile).wait_recv()
            far_send[h * 4 + tile] = (value + part_recv[h * 4 + tile].astype(F32)).astype(BF16)
            far_copy(h * 4 + tile).start()
    def stat_copy(n, to):
        return pltpu.make_async_remote_copy(
            src_ref=stat.at[0],
            dst_ref=stat.at[n],
            send_sem=st_s.at[n],
            recv_sem=st_r.at[n],
            device_id={"slab": to},
            device_id_type=MESH,
        )

    stat[0] = jnp.transpose(cols[3])[0:8]
    peers = ((1, partner), (2, far), (3, far_partner))
    for n, to in peers:
        stat_copy(n, to).start()
    for tile in range(4):
        mine_send[tile] = grad_tile(partner, tile, every).astype(BF16)
        mine_copy(tile).start()
    for tile in range(4):
        own[tile] = grad_tile(slab, tile, every)
    for n, to in peers:
        stat_copy(n, to).wait_recv()
    sums = stat[0] + stat[1] + stat[2] + stat[3]
    sums = jnp.transpose(jnp.concatenate([sums] * 16, axis=0))
    gate = cols[2, :, 0:1]
    gate_grad = sums[:, 0:1] * gate * (1.0 - gate)
    mean_one = sums[:, 1:2] * (1.0 / full)
    mean_two = sums[:, 2:3] * (1.0 / full)
    mean = cols[0, :, 0:1]
    inv = cols[1, :, 0:1]

    for tile in range(4):
        cs = pl.ds(tile * tile_w, tile_w)
        x = xf[slab, :, cs].astype(F32)
        cgrad_ref[:, cs] = jnp.sum(x * gate_grad, axis=0, keepdims=True)
        mine_copy(tile).wait_recv()
        own[tile] += mine_recv[tile].astype(F32)
    for tile in range(4):
        cs = pl.ds(tile * tile_w, tile_w)
        glob = pl.ds(pl.multiple_of(slab * width + tile * tile_w, tile_w), tile_w)
        gain_part = gain_ref[:, glob].astype(F32)
        cent_part = cent_ref[:, glob].astype(F32)
        for h in range(2):
            lo, up = h * half_rows, (h + 1) * half_rows
            hs = pl.ds(lo, half_rows)
            x = xf[slab, hs, cs].astype(F32)
            far_copy(h * 4 + tile).wait_recv()
            total = own[tile, hs, :] + far_recv[h * 4 + tile].astype(F32)
            scaled = total * gain_part
            hat = (x - mean[lo:up]) * inv[lo:up]
            value = inv[lo:up] * (scaled - mean_one[lo:up] - hat * mean_two[lo:up])
            value = value + gate_grad[lo:up] * cent_part
            yy[hs, cs] = value.astype(BF16)
        if tile == 1:
            pack(pg0, rg0, comp_t, yy, 0)
            send_all(pg0, rg0, 4)
    pack(pg1, rg1, comp_t, yy, 1)
    send_all(pg1, rg1, 5)
    wait_bytes(rg0, a2a_r.at[4])
    unpack(out_ref, (), pick_t, rg0, 0)
    wait_bytes(rg1, a2a_r.at[5])
    unpack(out_ref, (), pick_t, rg1, 1)

    for idx, buf in enumerate((px0, px1, pd0, pd1, pg0, pg1)):
        wait_bytes(buf, a2a_s.at[idx])
    for c in range(2):
        x_copy(c, slab, 0, far).wait_send()
        x_copy(c, slab, 1, partner).wait_send()
        x_copy(c, far, 2, partner).wait_send()
        for h in range(2):
            d_copy(h, c, slab, 0, far).wait_send()
            d_copy(h, c, slab, 1, partner).wait_send()
            d_copy(h, c, far, 2, partner).wait_send()
    for n in range(8):
        part_copy(n).wait_send()
        far_copy(n).wait_send()
    for n in range(4):
        mine_copy(n).wait_send()
    for n, to in peers:
        stat_copy(n, to).wait_send()


def hand_on(out_in, cgrad_in, out_ref, cgrad_ref):
    out_ref[...] = out_in[...]
    cgrad_ref[...] = cgrad_in[...]


def per_device(tokens, grad_out, position, centroid, gain, w_in, w_out):
    n_exp = lax.axis_size("expert")
    rows, width = tokens.shape
    full = centroid.shape[1]
    ff = w_in.shape[2]
    slots = n_exp * ROWS
    packed = 3 * width // 8
    vmem = pl.BlockSpec(memory_space=pltpu.VMEM)
    hbm = pl.BlockSpec(memory_space=pl.ANY)
    buf = pltpu.VMEM
    dma = pltpu.SemaphoreType.DMA
    shapes = (
        jax.ShapeDtypeStruct((rows, width), BF16),
        jax.ShapeDtypeStruct((1, width), F32),
    )
    out, cgrad = pl.pallas_call(
        functools.partial(kernel, n_exp),
        out_shape=shapes,
        in_specs=[vmem, vmem, vmem, hbm, hbm, hbm, hbm],
        out_specs=(vmem, vmem),
        scratch_shapes=[
            buf((rows, width), BF16),
            buf((rows, width), BF16),
            buf((full, ff), BF16),
            buf((ff, full), BF16),
            buf((4, slots, rows), BF16),
            buf((4, rows, slots), BF16),
            buf((slots, packed + 128), BF16),
            buf((slots, packed), BF16),
            buf((slots, packed), BF16),
            buf((slots, packed), BF16),
            buf((slots, packed + 128), BF16),
            buf((slots, packed), BF16),
            buf((slots, packed), BF16),
            buf((slots, packed), BF16),
            buf((4, rows, slots), BF16),
            buf((4, slots, rows), BF16),
            buf((N_SLAB, rows, width), BF16),
            buf((N_SLAB, rows, width), BF16),
            buf((N_SLAB, rows, width), BF16),
            buf((rows, ff), F32),
            buf((rows, ff), F32),
            buf((rows, ff), F32),
            buf((rows, ff), F32),
            buf((rows, ff), BF16),
            buf((8, ff), F32),
            buf((4, rows, 128), F32),
            buf((4, 8, rows), F32),
            buf((8, rows // 2, width // 4), BF16),
            buf((8, rows // 2, width // 4), BF16),
            buf((8, rows // 2, width // 4), BF16),
            buf((8, rows // 2, width // 4), BF16),
            buf((4, rows, width // 4), BF16),
            buf((4, rows, width // 4), BF16),
            buf((4, rows, width // 4), F32),
            buf((rows, width), BF16),
            buf((slots, packed), BF16),
            buf((slots, packed), BF16),
            buf((slots, packed), BF16),
            buf((slots, packed), BF16),
            dma((4,)),
            dma((6,)),
            dma((6,)),
            dma((18,)),
            dma((18,)),
            dma((20,)),
            dma((20,)),
            dma((4,)),
            dma((4,)),
        ],
        compiler_params=pltpu.CompilerParams(
            collective_id=0, has_side_effects=True, vmem_limit_bytes=56 * 2**20
        ),
        cost_estimate=pl.CostEstimate(
            flops=3 * 2 * rows * full * ff, bytes_accessed=4 * full * ff, transcendentals=rows * ff
        ),
    )(position.reshape(1, rows), centroid, gain, tokens, grad_out, w_in[0], w_out[0])
    return pl.pallas_call(
        hand_on,
        out_shape=shapes,
        in_specs=[vmem, vmem],
        out_specs=(vmem, vmem),
    )(out, cgrad)


def solution(mesh):
    placed = (
        P("expert", "slab"),
        P("expert", "slab"),
        P("expert"),
        P("expert", None),
        P("expert", None),
        P("expert", None, "slab"),
        P("expert", "slab", None),
    )
    return jax.shard_map(
        per_device,
        mesh=mesh,
        in_specs=placed,
        out_specs=(P("expert", "slab"), P("expert", "slab")),
        check_vma=False,
    )
```

```python
import functools
import math

import jax
import jax.numpy as jnp
from jax import lax
from jax.experimental import pallas as pl
from jax.experimental.pallas import tpu as pltpu
from jax.sharding import PartitionSpec as P

F32 = jnp.float32
BF16 = jnp.bfloat16
MESH = pl.DeviceIdType.MESH
ROWS = 16
ROOT = math.sqrt(2.0 / math.pi)
N_SLAB = 4


def iota(shape, dim):
    return lax.broadcasted_iota(jnp.int32, shape, dim)


def onehot(mask):
    return jnp.where(mask, 1.0, 0.0).astype(BF16)


def dot(a, b):
    return jnp.dot(a, b, preferred_element_type=F32)


def dot_t(a, b):
    return lax.dot_general(a, b, (((1,), (1,)), ((), ())), preferred_element_type=F32)


def kernel(
    n_exp,
    pos_ref,
    cent_ref,
    gain_ref,
    tok_hbm,
    dy_hbm,
    win_hbm,
    wout_hbm,
    out_ref,
    cgrad_ref,
    tok,
    gdy,
    win,
    wout,
    pick,
    pick_t,
    px0,
    px1,
    pd0,
    pd1,
    rx0,
    rx1,
    rd0,
    rd1,
    comp,
    comp_t,
    xf,
    df,
    nx,
    pre,
    act,
    slp,
    bk,
    delta,
    usum,
    cols,
    stat,
    part_send,
    part_recv,
    far_send,
    far_recv,
    mine_send,
    mine_recv,
    own,
    yy,
    pg0,
    pg1,
    rg0,
    rg1,
    lsem,
    a2a_s,
    a2a_r,
    ag_s,
    ag_r,
    rs_s,
    rs_r,
    st_s,
    st_r,
):
    rows, width = tok.shape
    full = N_SLAB * width
    ff = win.shape[1]
    half = width // 2
    q = half // 4
    tile_w = width // 4
    half_rows = rows // 2
    slots = n_exp * ROWS
    me = lax.axis_index("expert")
    slab = lax.axis_index("slab")
    hi, core = slab // 2, slab % 2
    partner = hi * 2 + (1 - core)
    far = (1 - hi) * 2 + core
    far_partner = (1 - hi) * 2 + (1 - core)

    cp_tok = pltpu.make_async_copy(tok_hbm, tok, lsem.at[0])
    cp_dy = pltpu.make_async_copy(dy_hbm, gdy, lsem.at[1])
    cp_win = pltpu.make_async_copy(win_hbm, win, lsem.at[2])
    cp_wout = pltpu.make_async_copy(wout_hbm, wout, lsem.at[3])
    cp_tok.start()
    cp_dy.start()

    bar = pltpu.get_barrier_semaphore()

    @pl.loop(1, n_exp)
    def _(k):
        pl.semaphore_signal(
            bar, inc=1, device_id={"expert": lax.rem(me + k, n_exp)}, device_id_type=MESH
        )

    for peer in (partner, far, far_partner):
        pl.semaphore_signal(bar, inc=1, device_id={"slab": peer}, device_id_type=MESH)
    cp_win.start()
    cp_wout.start()

    pos = pos_ref[...]
    tgt = lax.div(pos, rows)
    row = pos - tgt * rows
    hit = iota((n_exp, rows), 0) == tgt
    before = dot(onehot(hit), onehot(iota((rows, rows), 0) < iota((rows, rows), 1)))
    rank = jnp.sum(jnp.where(hit, before, 0.0), axis=0, keepdims=True).astype(jnp.int32)
    third = lax.shift_right_logical(rank * 11, 5)
    rem3 = rank - 3 * third
    slot = [tgt * ROWS + rank]
    for j in range(3):
        slot.append(jnp.where(rem3 == j, tgt * ROWS + 12 + third, -1))
    for k in range(4):
        pick[k] = onehot(iota((slots, rows), 0) == slot[k])

    row_one = jnp.broadcast_to((row + 1).astype(F32), (128, rows))
    meta = None
    for k in range(4):
        marks = jnp.where(iota((128, rows), 0) // 32 == k, row_one, 0.0).astype(BF16)
        term = dot_t(pick[k], marks)
        meta = term if meta is None else meta + term
    px0[:, pl.ds(3 * q, 128)] = meta.astype(BF16)

    mine = pl.ds(pl.multiple_of(me * ROWS, ROWS), ROWS)

    def pack(into, keep, take, source, c):
        last = source[:, pl.ds(c * half + 3 * q, q)]
        for j in range(3):
            cs = pl.ds(j * q, q)
            value = dot(take[0], source[:, pl.ds(c * half + j * q, q)]) + dot(take[1 + j], last)
            into[:, cs] = value.astype(BF16)
        keep[mine, :] = into[mine, :]

    def unpack(into, lead, take, source, c):
        into[lead + (slice(None), pl.ds(c * half, 3 * q))] = dot(
            take[0], source[:, pl.ds(0, 3 * q)]
        ).astype(BF16)
        value = dot(take[1], source[:, pl.ds(0, q)])
        value += dot(take[2], source[:, pl.ds(q, q)])
        value += dot(take[3], source[:, pl.ds(2 * q, q)])
        into[lead + (slice(None), pl.ds(c * half + 3 * q, q))] = value.astype(BF16)

    def send_all(source, target, idx):
        @pl.loop(1, n_exp)
        def _(k):
            d = lax.rem(me + k, n_exp)
            pltpu.make_async_remote_copy(
                src_ref=source.at[pl.ds(pl.multiple_of(d * ROWS, ROWS), ROWS)],
                dst_ref=target.at[mine],
                send_sem=a2a_s.at[idx],
                recv_sem=a2a_r.at[idx],
                device_id={"expert": d},
                device_id_type=MESH,
            ).start()

    def wait_bytes(ref, sem):
        part = ref.at[pl.ds(0, (n_exp - 1) * ROWS)]
        pltpu.make_async_copy(part, part, sem).wait()

    cp_tok.wait()
    pack(px0, rx0, pick, tok, 0)
    pl.semaphore_wait(bar, n_exp - 1 + 3)
    send_all(px0, rx0, 0)
    pack(px1, rx1, pick, tok, 1)
    send_all(px1, rx1, 1)
    cp_dy.wait()
    pack(pd0, rd0, pick, gdy, 0)
    pack(pd1, rd1, pick, gdy, 1)

    for k in range(4):
        turned = jnp.transpose(jnp.broadcast_to(slot[k].astype(F32), (128, rows)))[:, 0:1]
        pick_t[k] = onehot(iota((rows, slots), 1).astype(F32) == turned)
    cp_win.wait()
    gain_rows = jnp.broadcast_to(gain_ref[...], (16, full))

    @pl.loop(0, ff // 256)
    def _(n):
        cs = pl.ds(pl.multiple_of(n * 256, 256), 256)
        usum[:, cs] = dot(gain_rows, win[:, cs])[0:8]

    def gather_copy(buf, idx, rs, c, source, kind, to):
        block = buf.at[source, rs, pl.ds(c * half, half)]
        return pltpu.make_async_remote_copy(
            src_ref=block,
            dst_ref=block,
            send_sem=ag_s.at[idx * 3 + kind],
            recv_sem=ag_r.at[idx * 3 + kind],
            device_id={"slab": to},
            device_id_type=MESH,
        )

    every = pl.ds(0, rows)

    def x_copy(c, source, kind, to):
        return gather_copy(xf, c, every, c, source, kind, to)

    def d_copy(h, c, source, kind, to):
        return gather_copy(
            df, 2 + 2 * h + c, pl.ds(h * half_rows, half_rows), c, source, kind, to
        )

    def x_dense(recv, c):
        unpack(xf, (slab,), comp, recv, c)
        x_copy(c, slab, 0, far).start()
        x_copy(c, slab, 1, partner).start()

    def d_start(h, c):
        d_copy(h, c, slab, 0, far).start()
        d_copy(h, c, slab, 1, partner).start()

    wait_bytes(rx0, a2a_r.at[0])
    marks_in = rx0[:, pl.ds(3 * q, 128)].astype(F32)
    marks_t = jnp.transpose(marks_in)
    for k in range(4):
        comp[k] = onehot((iota((rows, slots), 0) + 1).astype(F32) == marks_t[32 * k : 32 * k + 1])
    x_dense(rx0, 0)
    send_all(pd0, rd0, 2)
    wait_bytes(rx1, a2a_r.at[1])
    x_dense(rx1, 1)
    send_all(pd1, rd1, 3)
    for k in range(4):
        comp_t[k] = onehot(
            (iota((slots, rows), 1) + 1).astype(F32) == marks_in[:, 32 * k : 32 * k + 1]
        )
    x_copy(0, far, 0, far).wait_recv()
    x_copy(0, far, 2, partner).start()
    wait_bytes(rd0, a2a_r.at[2])
    unpack(df, (slab,), comp, rd0, 0)
    d_start(0, 0)
    x_copy(1, far, 0, far).wait_recv()
    x_copy(1, far, 2, partner).start()
    wait_bytes(rd1, a2a_r.at[3])
    unpack(df, (slab,), comp, rd1, 1)
    d_start(0, 1)
    d_start(1, 0)
    d_start(1, 1)
    for c in range(2):
        x_copy(c, partner, 1, partner).wait_recv()
    for c in range(2):
        x_copy(c, far_partner, 2, partner).wait_recv()

    step = 16

    @pl.loop(0, rows // step, unroll=2)
    def _(i):
        rs = pl.ds(pl.multiple_of(i * step, step), step)
        xs = [xf[b, rs, :].astype(F32) for b in range(N_SLAB)]
        total = None
        logit = None
        for b in range(N_SLAB):
            c_b = cent_ref[:, pl.ds(b * width, width)].astype(F32)
            t_b = jnp.sum(xs[b], axis=1, keepdims=True)
            l_b = jnp.sum(xs[b] * c_b, axis=1, keepdims=True)
            total = t_b if total is None else total + t_b
            logit = l_b if logit is None else logit + l_b
        mean = total * (1.0 / full)
        spread = None
        for b in range(N_SLAB):
            xs[b] = xs[b] - mean
            v_b = jnp.sum(xs[b] * xs[b], axis=1, keepdims=True)
            spread = v_b if spread is None else spread + v_b
        inv = lax.rsqrt(spread * (1.0 / full) + 1e-05)
        for b in range(N_SLAB):
            g_b = gain_ref[:, pl.ds(b * width, width)].astype(F32)
            nx[b, rs, :] = (xs[b] * inv * g_b).astype(BF16)
        gate = 1.0 / (1.0 + jnp.exp(-logit))
        cols[0, rs, :] = jnp.broadcast_to(mean, (step, 128))
        cols[1, rs, :] = jnp.broadcast_to(inv, (step, 128))
        cols[2, rs, :] = jnp.broadcast_to(gate, (step, 128))
    for n in range(ff // 256):
        cs = pl.ds(n * 256, 256)
        acc = dot(nx[0], win[pl.ds(0, width), cs])
        for b in range(1, N_SLAB):
            acc += dot(nx[b], win[pl.ds(b * width, width), cs])
        pre[:, cs] = acc

    @pl.loop(0, rows // step, unroll=2)
    def _(i):
        rs = pl.ds(pl.multiple_of(i * step, step), step)
        p = pre[rs, :]
        gate = cols[2, rs, 0:1]
        sq = p * p
        tangent = jnp.tanh(ROOT * (p + 0.044715 * p * sq))
        mid = 0.5 * (1.0 + tangent)
        act[rs, :] = p * mid
        slp[rs, :] = gate * (
            mid + 0.5 * p * (1.0 - tangent * tangent) * ROOT * (1.0 + 3.0 * 0.044715 * sq)
        )

    cp_wout.wait()

    def back_from(h, sources, first):
        hs = pl.ds(h * half_rows, half_rows)

        for n in range(ff // 256):
            rs = pl.ds(n * 256, 256)
            value = None
            for b in sources:
                base = pl.multiple_of(b * width, width)
                term = dot_t(df[b, hs, :], wout[rs, pl.ds(base, width)])
                value = term if value is None else value + term
            if first:
                bk[hs, rs] = value
            else:
                bk[hs, rs] += value

    def grad_tile(b, tile, rs):
        base = pl.multiple_of(b * width + tile * tile_w, tile_w)
        return dot_t(delta[rs, :], win[pl.ds(base, tile_w), :])

    def reduce_copy(kind, n, src, dst, to):
        return pltpu.make_async_remote_copy(
            src_ref=src.at[n],
            dst_ref=dst.at[n],
            send_sem=rs_s.at[kind * 8 + n],
            recv_sem=rs_r.at[kind * 8 + n],
            device_id={"slab": to},
            device_id_type=MESH,
        )

    def part_copy(n):
        return reduce_copy(0, n, part_send, part_recv, partner)

    def far_copy(n):
        return reduce_copy(1, n, far_send, far_recv, far)

    def mine_copy(n):
        return reduce_copy(2, n, mine_send, mine_recv, partner)

    def forward(h):
        for c in range(2):
            d_copy(h, c, far, 0, far).wait_recv()
            d_copy(h, c, far, 2, partner).start()

    def arrived(h, source, kind):
        for c in range(2):
            d_copy(h, c, source, kind, partner).wait_recv()

    def delta_of(h):
        @pl.loop(0, half_rows // step, unroll=4)
        def _(i):
            rs = pl.ds(pl.multiple_of(h * half_rows + i * step, step), step)
            b = bk[rs, :]
            d = (b * slp[rs, :]).astype(BF16)
            delta[rs, :] = d
            d = d.astype(F32)
            g_sum = jnp.sum(act[rs, :] * b, axis=1, keepdims=True)
            one = jnp.sum(d * usum[0:1, :], axis=1, keepdims=True)
            two = jnp.sum(d * pre[rs, :], axis=1, keepdims=True)
            lane = iota((step, 128), 1)
            cols[3, rs, :] = jnp.where(lane == 0, g_sum, jnp.where(lane == 1, one, two))

    def parts(h):
        hs = pl.ds(h * half_rows, half_rows)
        for tile in range(4):
            part_send[h * 4 + tile] = grad_tile(far_partner, tile, hs).astype(BF16)
            part_copy(h * 4 + tile).start()

    def fars(h):
        hs = pl.ds(h * half_rows, half_rows)
        for tile in range(4):
            value = grad_tile(far, tile, hs)
            part_copy(h * 4 + tile).wait_recv()
            far_send[h * 4 + tile] = (value + part_recv[h * 4 + tile].astype(F32)).astype(BF16)
            far_copy(h * 4 + tile).start()

    def stat_copy(n, to):
        return pltpu.make_async_remote_copy(
            src_ref=stat.at[0],
            dst_ref=stat.at[n],
            send_sem=st_s.at[n],
            recv_sem=st_r.at[n],
            device_id={"slab": to},
            device_id_type=MESH,
        )

    arrived(0, partner, 1)
    back_from(0, (slab, partner), True)
    forward(0)
    back_from(0, (far,), False)
    arrived(0, far_partner, 2)
    back_from(0, (far_partner,), False)
    delta_of(0)
    parts(0)
    arrived(1, partner, 1)
    forward(1)
    back_from(1, (slab, partner, far), True)
    fars(0)
    arrived(1, far_partner, 2)
    back_from(1, (far_partner,), False)
    delta_of(1)
    parts(1)
    stat[0] = jnp.transpose(cols[3])[0:8]
    peers = ((1, partner), (2, far), (3, far_partner))
    for n, to in peers:
        stat_copy(n, to).start()
    for tile in range(4):
        mine_send[tile] = grad_tile(partner, tile, every).astype(BF16)
        mine_copy(tile).start()
    fars(1)
    for tile in range(4):
        own[tile] = grad_tile(slab, tile, every)
    for n, to in peers:
        stat_copy(n, to).wait_recv()
    sums = stat[0] + stat[1] + stat[2] + stat[3]
    sums = jnp.transpose(jnp.concatenate([sums] * 16, axis=0))
    gate = cols[2, :, 0:1]
    gate_grad = sums[:, 0:1] * gate * (1.0 - gate)
    mean_one = sums[:, 1:2] * (1.0 / full)
    mean_two = sums[:, 2:3] * (1.0 / full)
    mean = cols[0, :, 0:1]
    inv = cols[1, :, 0:1]

    for tile in range(4):
        cs = pl.ds(tile * tile_w, tile_w)
        x = xf[slab, :, cs].astype(F32)
        cgrad_ref[:, cs] = jnp.sum(x * gate_grad, axis=0, keepdims=True)
        mine_copy(tile).wait_recv()
        own[tile] += mine_recv[tile].astype(F32)
    for tile in range(4):
        cs = pl.ds(tile * tile_w, tile_w)
        glob = pl.ds(pl.multiple_of(slab * width + tile * tile_w, tile_w), tile_w)
        gain_part = gain_ref[:, glob].astype(F32)
        cent_part = cent_ref[:, glob].astype(F32)
        for h in range(2):
            lo, up = h * half_rows, (h + 1) * half_rows
            hs = pl.ds(lo, half_rows)
            x = xf[slab, hs, cs].astype(F32)
            far_copy(h * 4 + tile).wait_recv()
            total = own[tile, hs, :] + far_recv[h * 4 + tile].astype(F32)
            scaled = total * gain_part
            hat = (x - mean[lo:up]) * inv[lo:up]
            value = inv[lo:up] * (scaled - mean_one[lo:up] - hat * mean_two[lo:up])
            value = value + gate_grad[lo:up] * cent_part
            yy[hs, cs] = value.astype(BF16)
        if tile == 1:
            pack(pg0, rg0, comp_t, yy, 0)
            send_all(pg0, rg0, 4)
    pack(pg1, rg1, comp_t, yy, 1)
    send_all(pg1, rg1, 5)
    wait_bytes(rg0, a2a_r.at[4])
    unpack(out_ref, (), pick_t, rg0, 0)
    wait_bytes(rg1, a2a_r.at[5])
    unpack(out_ref, (), pick_t, rg1, 1)

    for idx, buf in enumerate((px0, px1, pd0, pd1, pg0, pg1)):
        wait_bytes(buf, a2a_s.at[idx])
    for c in range(2):
        x_copy(c, slab, 0, far).wait_send()
        x_copy(c, slab, 1, partner).wait_send()
        x_copy(c, far, 2, partner).wait_send()
        for h in range(2):
            d_copy(h, c, slab, 0, far).wait_send()
            d_copy(h, c, slab, 1, partner).wait_send()
            d_copy(h, c, far, 2, partner).wait_send()
    for n in range(8):
        part_copy(n).wait_send()
        far_copy(n).wait_send()
    for n in range(4):
        mine_copy(n).wait_send()
    for n, to in peers:
        stat_copy(n, to).wait_send()


def hand_on(out_in, cgrad_in, out_ref, cgrad_ref):
    out_ref[...] = out_in[...]
    cgrad_ref[...] = cgrad_in[...]


def per_device(tokens, grad_out, position, centroid, gain, w_in, w_out):
    n_exp = lax.axis_size("expert")
    rows, width = tokens.shape
    full = centroid.shape[1]
    ff = w_in.shape[2]
    slots = n_exp * ROWS
    packed = 3 * width // 8
    vmem = pl.BlockSpec(memory_space=pltpu.VMEM)
    hbm = pl.BlockSpec(memory_space=pl.ANY)
    buf = pltpu.VMEM
    dma = pltpu.SemaphoreType.DMA
    shapes = (
        jax.ShapeDtypeStruct((rows, width), BF16),
        jax.ShapeDtypeStruct((1, width), F32),
    )
    out, cgrad = pl.pallas_call(
        functools.partial(kernel, n_exp),
        out_shape=shapes,
        in_specs=[vmem, vmem, vmem, hbm, hbm, hbm, hbm],
        out_specs=(vmem, vmem),
        scratch_shapes=[
            buf((rows, width), BF16),
            buf((rows, width), BF16),
            buf((full, ff), BF16),
            buf((ff, full), BF16),
            buf((4, slots, rows), BF16),
            buf((4, rows, slots), BF16),
            buf((slots, packed + 128), BF16),
            buf((slots, packed), BF16),
            buf((slots, packed), BF16),
            buf((slots, packed), BF16),
            buf((slots, packed + 128), BF16),
            buf((slots, packed), BF16),
            buf((slots, packed), BF16),
            buf((slots, packed), BF16),
            buf((4, rows, slots), BF16),
            buf((4, slots, rows), BF16),
            buf((N_SLAB, rows, width), BF16),
            buf((N_SLAB, rows, width), BF16),
            buf((N_SLAB, rows, width), BF16),
            buf((rows, ff), F32),
            buf((rows, ff), F32),
            buf((rows, ff), F32),
            buf((rows, ff), F32),
            buf((rows, ff), BF16),
            buf((8, ff), F32),
            buf((4, rows, 128), F32),
            buf((4, 8, rows), F32),
            buf((8, rows // 2, width // 4), BF16),
            buf((8, rows // 2, width // 4), BF16),
            buf((8, rows // 2, width // 4), BF16),
            buf((8, rows // 2, width // 4), BF16),
            buf((4, rows, width // 4), BF16),
            buf((4, rows, width // 4), BF16),
            buf((4, rows, width // 4), F32),
            buf((rows, width), BF16),
            buf((slots, packed), BF16),
            buf((slots, packed), BF16),
            buf((slots, packed), BF16),
            buf((slots, packed), BF16),
            dma((4,)),
            dma((6,)),
            dma((6,)),
            dma((18,)),
            dma((18,)),
            dma((20,)),
            dma((20,)),
            dma((4,)),
            dma((4,)),
        ],
        compiler_params=pltpu.CompilerParams(
            collective_id=0, has_side_effects=True, vmem_limit_bytes=56 * 2**20
        ),
        cost_estimate=pl.CostEstimate(
            flops=3 * 2 * rows * full * ff, bytes_accessed=4 * full * ff, transcendentals=rows * ff
        ),
    )(position.reshape(1, rows), centroid, gain, tokens, grad_out, w_in[0], w_out[0])
    return pl.pallas_call(
        hand_on,
        out_shape=shapes,
        in_specs=[vmem, vmem],
        out_specs=(vmem, vmem),
    )(out, cgrad)


def solution(mesh):
    placed = (
        P("expert", "slab"),
        P("expert", "slab"),
        P("expert"),
        P("expert", None),
        P("expert", None),
        P("expert", None, "slab"),
        P("expert", "slab", None),
    )
    return jax.shard_map(
        per_device,
        mesh=mesh,
        in_specs=placed,
        out_specs=(P("expert", "slab"), P("expert", "slab")),
        check_vma=False,
    )
```

```python
import functools
import math

import jax
import jax.numpy as jnp
from jax import lax
from jax.experimental import pallas as pl
from jax.experimental.pallas import tpu as pltpu
from jax.sharding import PartitionSpec as P

F32 = jnp.float32
BF16 = jnp.bfloat16
MESH = pl.DeviceIdType.MESH
ROWS = 16
ROOT = math.sqrt(2.0 / math.pi)
N_SLAB = 4


def iota(shape, dim):
    return lax.broadcasted_iota(jnp.int32, shape, dim)


def onehot(mask):
    return jnp.where(mask, 1.0, 0.0).astype(BF16)


def dot(a, b):
    return jnp.dot(a, b, preferred_element_type=F32)


def dot_t(a, b):
    return lax.dot_general(a, b, (((1,), (1,)), ((), ())), preferred_element_type=F32)


def kernel(
    n_exp,
    pos_ref,
    cent_ref,
    gain_ref,
    tok_hbm,
    dy_hbm,
    win_hbm,
    wout_hbm,
    out_ref,
    cgrad_ref,
    tok,
    gdy,
    win,
    wout,
    pick,
    pick_t,
    px0,
    px1,
    pd0,
    pd1,
    rx0,
    rx1,
    rd0,
    rd1,
    comp,
    comp_t,
    xf,
    df,
    nx,
    pre,
    act,
    slp,
    bk,
    delta,
    usum,
    cols,
    stat,
    part_send,
    part_recv,
    far_send,
    far_recv,
    mine_send,
    mine_recv,
    own,
    yy,
    pg0,
    pg1,
    rg0,
    rg1,
    lsem,
    a2a_s,
    a2a_r,
    ag_s,
    ag_r,
    rs_s,
    rs_r,
    st_s,
    st_r,
):
    rows, width = tok.shape
    full = N_SLAB * width
    ff = win.shape[1]
    half = width // 2
    q = half // 4
    tile_w = width // 4
    half_rows = rows // 2
    slots = n_exp * ROWS
    me = lax.axis_index("expert")
    slab = lax.axis_index("slab")
    hi, core = slab // 2, slab % 2
    partner = hi * 2 + (1 - core)
    far = (1 - hi) * 2 + core
    far_partner = (1 - hi) * 2 + (1 - core)

    cp_tok = pltpu.make_async_copy(tok_hbm, tok, lsem.at[0])
    cp_dy = pltpu.make_async_copy(dy_hbm, gdy, lsem.at[1])
    cp_win = pltpu.make_async_copy(win_hbm, win, lsem.at[2])
    cp_wout = pltpu.make_async_copy(wout_hbm, wout, lsem.at[3])
    cp_tok.start()
    cp_dy.start()

    bar = pltpu.get_barrier_semaphore()

    @pl.loop(1, n_exp)
    def _(k):
        pl.semaphore_signal(
            bar, inc=1, device_id={"expert": lax.rem(me + k, n_exp)}, device_id_type=MESH
        )

    for peer in (partner, far, far_partner):
        pl.semaphore_signal(bar, inc=1, device_id={"slab": peer}, device_id_type=MESH)
    cp_win.start()
    cp_wout.start()

    pos = pos_ref[...]
    tgt = lax.div(pos, rows)
    row = pos - tgt * rows
    hit = iota((n_exp, rows), 0) == tgt
    before = dot(onehot(hit), onehot(iota((rows, rows), 0) < iota((rows, rows), 1)))
    rank = jnp.sum(jnp.where(hit, before, 0.0), axis=0, keepdims=True).astype(jnp.int32)
    third = lax.shift_right_logical(rank * 11, 5)
    rem3 = rank - 3 * third
    slot = [tgt * ROWS + rank]
    for j in range(3):
        slot.append(jnp.where(rem3 == j, tgt * ROWS + 12 + third, -1))
    for k in range(4):
        pick[k] = onehot(iota((slots, rows), 0) == slot[k])

    row_one = jnp.broadcast_to((row + 1).astype(F32), (128, rows))
    meta = None
    for k in range(4):
        marks = jnp.where(iota((128, rows), 0) // 32 == k, row_one, 0.0).astype(BF16)
        term = dot_t(pick[k], marks)
        meta = term if meta is None else meta + term
    px0[:, pl.ds(3 * q, 128)] = meta.astype(BF16)

    mine = pl.ds(pl.multiple_of(me * ROWS, ROWS), ROWS)

    def pack(into, keep, take, source, c):
        last = source[:, pl.ds(c * half + 3 * q, q)]
        for j in range(3):
            cs = pl.ds(j * q, q)
            value = dot(take[0], source[:, pl.ds(c * half + j * q, q)]) + dot(take[1 + j], last)
            into[:, cs] = value.astype(BF16)
        keep[mine, :] = into[mine, :]

    def unpack(into, lead, take, source, c):
        into[lead + (slice(None), pl.ds(c * half, 3 * q))] = dot(
            take[0], source[:, pl.ds(0, 3 * q)]
        ).astype(BF16)
        value = dot(take[1], source[:, pl.ds(0, q)])
        value += dot(take[2], source[:, pl.ds(q, q)])
        value += dot(take[3], source[:, pl.ds(2 * q, q)])
        into[lead + (slice(None), pl.ds(c * half + 3 * q, q))] = value.astype(BF16)

    def send_all(source, target, idx):
        @pl.loop(1, n_exp)
        def _(k):
            d = lax.rem(me + k, n_exp)
            pltpu.make_async_remote_copy(
                src_ref=source.at[pl.ds(pl.multiple_of(d * ROWS, ROWS), ROWS)],
                dst_ref=target.at[mine],
                send_sem=a2a_s.at[idx],
                recv_sem=a2a_r.at[idx],
                device_id={"expert": d},
                device_id_type=MESH,
            ).start()

    def wait_bytes(ref, sem):
        part = ref.at[pl.ds(0, (n_exp - 1) * ROWS)]
        pltpu.make_async_copy(part, part, sem).wait()

    cp_tok.wait()
    pack(px0, rx0, pick, tok, 0)
    pl.semaphore_wait(bar, n_exp - 1 + 3)
    send_all(px0, rx0, 0)
    pack(px1, rx1, pick, tok, 1)
    send_all(px1, rx1, 1)
    cp_dy.wait()
    pack(pd0, rd0, pick, gdy, 0)
    pack(pd1, rd1, pick, gdy, 1)

    for k in range(4):
        turned = jnp.transpose(jnp.broadcast_to(slot[k].astype(F32), (128, rows)))[:, 0:1]
        pick_t[k] = onehot(iota((rows, slots), 1).astype(F32) == turned)
    cp_win.wait()
    gain_rows = jnp.broadcast_to(gain_ref[...], (16, full))

    @pl.loop(0, ff // 256)
    def _(n):
        cs = pl.ds(pl.multiple_of(n * 256, 256), 256)
        usum[:, cs] = dot(gain_rows, win[:, cs])[0:8]

    def gather_copy(buf, idx, rs, c, source, kind, to):
        block = buf.at[source, rs, pl.ds(c * half, half)]
        return pltpu.make_async_remote_copy(
            src_ref=block,
            dst_ref=block,
            send_sem=ag_s.at[idx * 3 + kind],
            recv_sem=ag_r.at[idx * 3 + kind],
            device_id={"slab": to},
            device_id_type=MESH,
        )

    every = pl.ds(0, rows)

    def x_copy(c, source, kind, to):
        return gather_copy(xf, c, every, c, source, kind, to)

    def d_copy(h, c, source, kind, to):
        return gather_copy(
            df, 2 + 2 * h + c, pl.ds(h * half_rows, half_rows), c, source, kind, to
        )

    def x_dense(recv, c):
        unpack(xf, (slab,), comp, recv, c)
        x_copy(c, slab, 0, far).start()
        x_copy(c, slab, 1, partner).start()

    def d_start(h, c):
        d_copy(h, c, slab, 0, far).start()
        d_copy(h, c, slab, 1, partner).start()

    wait_bytes(rx0, a2a_r.at[0])
    marks_in = rx0[:, pl.ds(3 * q, 128)].astype(F32)
    marks_t = jnp.transpose(marks_in)
    for k in range(4):
        comp[k] = onehot((iota((rows, slots), 0) + 1).astype(F32) == marks_t[32 * k : 32 * k + 1])
    x_dense(rx0, 0)
    send_all(pd0, rd0, 2)
    wait_bytes(rx1, a2a_r.at[1])
    x_dense(rx1, 1)
    send_all(pd1, rd1, 3)
    for k in range(4):
        comp_t[k] = onehot(
            (iota((slots, rows), 1) + 1).astype(F32) == marks_in[:, 32 * k : 32 * k + 1]
        )
    x_copy(0, far, 0, far).wait_recv()
    x_copy(0, far, 2, partner).start()
    wait_bytes(rd0, a2a_r.at[2])
    unpack(df, (slab,), comp, rd0, 0)
    d_start(0, 0)
    x_copy(1, far, 0, far).wait_recv()
    x_copy(1, far, 2, partner).start()
    wait_bytes(rd1, a2a_r.at[3])
    unpack(df, (slab,), comp, rd1, 1)
    d_start(0, 1)
    d_start(1, 0)
    d_start(1, 1)
    for c in range(2):
        x_copy(c, partner, 1, partner).wait_recv()
    for c in range(2):
        x_copy(c, far_partner, 2, partner).wait_recv()

    step = 16

    @pl.loop(0, rows // step, unroll=2)
    def _(i):
        rs = pl.ds(pl.multiple_of(i * step, step), step)
        xs = [xf[b, rs, :].astype(F32) for b in range(N_SLAB)]
        total = None
        logit = None
        for b in range(N_SLAB):
            c_b = cent_ref[:, pl.ds(b * width, width)].astype(F32)
            t_b = jnp.sum(xs[b], axis=1, keepdims=True)
            l_b = jnp.sum(xs[b] * c_b, axis=1, keepdims=True)
            total = t_b if total is None else total + t_b
            logit = l_b if logit is None else logit + l_b
        mean = total * (1.0 / full)
        spread = None
        for b in range(N_SLAB):
            xs[b] = xs[b] - mean
            v_b = jnp.sum(xs[b] * xs[b], axis=1, keepdims=True)
            spread = v_b if spread is None else spread + v_b
        inv = lax.rsqrt(spread * (1.0 / full) + 1e-05)
        for b in range(N_SLAB):
            g_b = gain_ref[:, pl.ds(b * width, width)].astype(F32)
            nx[b, rs, :] = (xs[b] * inv * g_b).astype(BF16)
        gate = 1.0 / (1.0 + jnp.exp(-logit))
        cols[0, rs, :] = jnp.broadcast_to(mean, (step, 128))
        cols[1, rs, :] = jnp.broadcast_to(inv, (step, 128))
        cols[2, rs, :] = jnp.broadcast_to(gate, (step, 128))
    for n in range(ff // 256):
        cs = pl.ds(n * 256, 256)
        acc = dot(nx[0], win[pl.ds(0, width), cs])
        for b in range(1, N_SLAB):
            acc += dot(nx[b], win[pl.ds(b * width, width), cs])
        pre[:, cs] = acc

    @pl.loop(0, rows // step, unroll=2)
    def _(i):
        rs = pl.ds(pl.multiple_of(i * step, step), step)
        p = pre[rs, :]
        gate = cols[2, rs, 0:1]
        sq = p * p
        tangent = jnp.tanh(ROOT * (p + 0.044715 * p * sq))
        mid = 0.5 * (1.0 + tangent)
        act[rs, :] = p * mid
        slp[rs, :] = gate * (
            mid + 0.5 * p * (1.0 - tangent * tangent) * ROOT * (1.0 + 3.0 * 0.044715 * sq)
        )

    cp_wout.wait()

    def back_from(h, sources, first):
        hs = pl.ds(h * half_rows, half_rows)

        for n in range(ff // 256):
            rs = pl.ds(n * 256, 256)
            value = None
            for b in sources:
                base = pl.multiple_of(b * width, width)
                term = dot_t(df[b, hs, :], wout[rs, pl.ds(base, width)])
                value = term if value is None else value + term
            if first:
                bk[hs, rs] = value
            else:
                bk[hs, rs] += value

    def grad_tile(b, tile, rs):
        base = pl.multiple_of(b * width + tile * tile_w, tile_w)
        return dot_t(delta[rs, :], win[pl.ds(base, tile_w), :])

    def reduce_copy(kind, n, src, dst, to):
        return pltpu.make_async_remote_copy(
            src_ref=src.at[n],
            dst_ref=dst.at[n],
            send_sem=rs_s.at[kind * 8 + n],
            recv_sem=rs_r.at[kind * 8 + n],
            device_id={"slab": to},
            device_id_type=MESH,
        )

    def part_copy(n):
        return reduce_copy(0, n, part_send, part_recv, partner)

    def far_copy(n):
        return reduce_copy(1, n, far_send, far_recv, far)

    def mine_copy(n):
        return reduce_copy(2, n, mine_send, mine_recv, partner)

    def forward(h):
        for c in range(2):
            d_copy(h, c, far, 0, far).wait_recv()
            d_copy(h, c, far, 2, partner).start()

    def arrived(h, source, kind):
        for c in range(2):
            d_copy(h, c, source, kind, partner).wait_recv()

    def delta_of(h):
        @pl.loop(0, half_rows // step, unroll=4)
        def _(i):
            rs = pl.ds(pl.multiple_of(h * half_rows + i * step, step), step)
            b = bk[rs, :]
            d = (b * slp[rs, :]).astype(BF16)
            delta[rs, :] = d
            d = d.astype(F32)
            g_sum = jnp.sum(act[rs, :] * b, axis=1, keepdims=True)
            one = jnp.sum(d * usum[0:1, :], axis=1, keepdims=True)
            two = jnp.sum(d * pre[rs, :], axis=1, keepdims=True)
            lane = iota((step, 128), 1)
            cols[3, rs, :] = jnp.where(lane == 0, g_sum, jnp.where(lane == 1, one, two))

    def parts(h):
        hs = pl.ds(h * half_rows, half_rows)
        for tile in range(4):
            part_send[h * 4 + tile] = grad_tile(far_partner, tile, hs).astype(BF16)
            part_copy(h * 4 + tile).start()

    def fars(h):
        hs = pl.ds(h * half_rows, half_rows)
        for tile in range(4):
            value = grad_tile(far, tile, hs)
            part_copy(h * 4 + tile).wait_recv()
            far_send[h * 4 + tile] = (value + part_recv[h * 4 + tile].astype(F32)).astype(BF16)
            far_copy(h * 4 + tile).start()

    def stat_copy(n, to):
        return pltpu.make_async_remote_copy(
            src_ref=stat.at[0],
            dst_ref=stat.at[n],
            send_sem=st_s.at[n],
            recv_sem=st_r.at[n],
            device_id={"slab": to},
            device_id_type=MESH,
        )

    arrived(0, partner, 1)
    back_from(0, (slab, partner), True)
    forward(0)
    back_from(0, (far,), False)
    arrived(0, far_partner, 2)
    back_from(0, (far_partner,), False)
    delta_of(0)
    parts(0)
    arrived(1, partner, 1)
    forward(1)
    back_from(1, (slab, partner, far), True)
    fars(0)
    arrived(1, far_partner, 2)
    back_from(1, (far_partner,), False)
    delta_of(1)
    parts(1)
    stat[0] = jnp.transpose(cols[3])[0:8]
    peers = ((1, partner), (2, far), (3, far_partner))
    for n, to in peers:
        stat_copy(n, to).start()
    fars(1)
    for tile in range(4):
        mine_send[tile] = grad_tile(partner, tile, every).astype(BF16)
        mine_copy(tile).start()
    for tile in range(4):
        own[tile] = grad_tile(slab, tile, every)
    for n, to in peers:
        stat_copy(n, to).wait_recv()
    sums = stat[0] + stat[1] + stat[2] + stat[3]
    sums = jnp.transpose(jnp.concatenate([sums] * 16, axis=0))
    gate = cols[2, :, 0:1]
    gate_grad = sums[:, 0:1] * gate * (1.0 - gate)
    mean_one = sums[:, 1:2] * (1.0 / full)
    mean_two = sums[:, 2:3] * (1.0 / full)
    mean = cols[0, :, 0:1]
    inv = cols[1, :, 0:1]

    for tile in range(4):
        cs = pl.ds(tile * tile_w, tile_w)
        x = xf[slab, :, cs].astype(F32)
        cgrad_ref[:, cs] = jnp.sum(x * gate_grad, axis=0, keepdims=True)
        mine_copy(tile).wait_recv()
        own[tile] += mine_recv[tile].astype(F32)
    for tile in range(4):
        cs = pl.ds(tile * tile_w, tile_w)
        glob = pl.ds(pl.multiple_of(slab * width + tile * tile_w, tile_w), tile_w)
        gain_part = gain_ref[:, glob].astype(F32)
        cent_part = cent_ref[:, glob].astype(F32)
        for h in range(2):
            lo, up = h * half_rows, (h + 1) * half_rows
            hs = pl.ds(lo, half_rows)
            x = xf[slab, hs, cs].astype(F32)
            far_copy(h * 4 + tile).wait_recv()
            total = own[tile, hs, :] + far_recv[h * 4 + tile].astype(F32)
            scaled = total * gain_part
            hat = (x - mean[lo:up]) * inv[lo:up]
            value = inv[lo:up] * (scaled - mean_one[lo:up] - hat * mean_two[lo:up])
            value = value + gate_grad[lo:up] * cent_part
            yy[hs, cs] = value.astype(BF16)
        if tile == 1:
            pack(pg0, rg0, comp_t, yy, 0)
            send_all(pg0, rg0, 4)
    pack(pg1, rg1, comp_t, yy, 1)
    send_all(pg1, rg1, 5)
    wait_bytes(rg0, a2a_r.at[4])
    unpack(out_ref, (), pick_t, rg0, 0)
    wait_bytes(rg1, a2a_r.at[5])
    unpack(out_ref, (), pick_t, rg1, 1)

    for idx, buf in enumerate((px0, px1, pd0, pd1, pg0, pg1)):
        wait_bytes(buf, a2a_s.at[idx])
    for c in range(2):
        x_copy(c, slab, 0, far).wait_send()
        x_copy(c, slab, 1, partner).wait_send()
        x_copy(c, far, 2, partner).wait_send()
        for h in range(2):
            d_copy(h, c, slab, 0, far).wait_send()
            d_copy(h, c, slab, 1, partner).wait_send()
            d_copy(h, c, far, 2, partner).wait_send()
    for n in range(8):
        part_copy(n).wait_send()
        far_copy(n).wait_send()
    for n in range(4):
        mine_copy(n).wait_send()
    for n, to in peers:
        stat_copy(n, to).wait_send()


def hand_on(out_in, cgrad_in, out_ref, cgrad_ref):
    out_ref[...] = out_in[...]
    cgrad_ref[...] = cgrad_in[...]


def per_device(tokens, grad_out, position, centroid, gain, w_in, w_out):
    n_exp = lax.axis_size("expert")
    rows, width = tokens.shape
    full = centroid.shape[1]
    ff = w_in.shape[2]
    slots = n_exp * ROWS
    packed = 3 * width // 8
    vmem = pl.BlockSpec(memory_space=pltpu.VMEM)
    hbm = pl.BlockSpec(memory_space=pl.ANY)
    buf = pltpu.VMEM
    dma = pltpu.SemaphoreType.DMA
    shapes = (
        jax.ShapeDtypeStruct((rows, width), BF16),
        jax.ShapeDtypeStruct((1, width), F32),
    )
    out, cgrad = pl.pallas_call(
        functools.partial(kernel, n_exp),
        out_shape=shapes,
        in_specs=[vmem, vmem, vmem, hbm, hbm, hbm, hbm],
        out_specs=(vmem, vmem),
        scratch_shapes=[
            buf((rows, width), BF16),
            buf((rows, width), BF16),
            buf((full, ff), BF16),
            buf((ff, full), BF16),
            buf((4, slots, rows), BF16),
            buf((4, rows, slots), BF16),
            buf((slots, packed + 128), BF16),
            buf((slots, packed), BF16),
            buf((slots, packed), BF16),
            buf((slots, packed), BF16),
            buf((slots, packed + 128), BF16),
            buf((slots, packed), BF16),
            buf((slots, packed), BF16),
            buf((slots, packed), BF16),
            buf((4, rows, slots), BF16),
            buf((4, slots, rows), BF16),
            buf((N_SLAB, rows, width), BF16),
            buf((N_SLAB, rows, width), BF16),
            buf((N_SLAB, rows, width), BF16),
            buf((rows, ff), F32),
            buf((rows, ff), F32),
            buf((rows, ff), F32),
            buf((rows, ff), F32),
            buf((rows, ff), BF16),
            buf((8, ff), F32),
            buf((4, rows, 128), F32),
            buf((4, 8, rows), F32),
            buf((8, rows // 2, width // 4), BF16),
            buf((8, rows // 2, width // 4), BF16),
            buf((8, rows // 2, width // 4), BF16),
            buf((8, rows // 2, width // 4), BF16),
            buf((4, rows, width // 4), BF16),
            buf((4, rows, width // 4), BF16),
            buf((4, rows, width // 4), F32),
            buf((rows, width), BF16),
            buf((slots, packed), BF16),
            buf((slots, packed), BF16),
            buf((slots, packed), BF16),
            buf((slots, packed), BF16),
            dma((4,)),
            dma((6,)),
            dma((6,)),
            dma((18,)),
            dma((18,)),
            dma((20,)),
            dma((20,)),
            dma((4,)),
            dma((4,)),
        ],
        compiler_params=pltpu.CompilerParams(
            collective_id=0, has_side_effects=True, vmem_limit_bytes=56 * 2**20
        ),
        cost_estimate=pl.CostEstimate(
            flops=3 * 2 * rows * full * ff, bytes_accessed=4 * full * ff, transcendentals=rows * ff
        ),
    )(position.reshape(1, rows), centroid, gain, tokens, grad_out, w_in[0], w_out[0])
    return pl.pallas_call(
        hand_on,
        out_shape=shapes,
        in_specs=[vmem, vmem],
        out_specs=(vmem, vmem),
    )(out, cgrad)


def solution(mesh):
    placed = (
        P("expert", "slab"),
        P("expert", "slab"),
        P("expert"),
        P("expert", None),
        P("expert", None),
        P("expert", None, "slab"),
        P("expert", "slab", None),
    )
    return jax.shard_map(
        per_device,
        mesh=mesh,
        in_specs=placed,
        out_specs=(P("expert", "slab"), P("expert", "slab")),
        check_vma=False,
    )
```

```python
import functools
import math

import jax
import jax.numpy as jnp
from jax import lax
from jax.experimental import pallas as pl
from jax.experimental.pallas import tpu as pltpu
from jax.sharding import PartitionSpec as P

F32 = jnp.float32
BF16 = jnp.bfloat16
MESH = pl.DeviceIdType.MESH
ROWS = 16
ROOT = math.sqrt(2.0 / math.pi)
N_SLAB = 4


def iota(shape, dim):
    return lax.broadcasted_iota(jnp.int32, shape, dim)


def onehot(mask):
    return jnp.where(mask, 1.0, 0.0).astype(BF16)


def dot(a, b):
    return jnp.dot(a, b, preferred_element_type=F32)


def dot_t(a, b):
    return lax.dot_general(a, b, (((1,), (1,)), ((), ())), preferred_element_type=F32)


def kernel(
    n_exp,
    pos_ref,
    cent_ref,
    gain_ref,
    tok_hbm,
    dy_hbm,
    win_hbm,
    wout_hbm,
    out_ref,
    cgrad_ref,
    tok,
    gdy,
    win,
    wout,
    pick,
    pick_t,
    px0,
    px1,
    pd0,
    pd1,
    rx0,
    rx1,
    rd0,
    rd1,
    comp,
    comp_t,
    xf,
    df,
    nx,
    pre,
    act,
    slp,
    bk,
    delta,
    usum,
    cols,
    stat,
    part_send,
    part_recv,
    far_send,
    far_recv,
    mine_send,
    mine_recv,
    own,
    yy,
    pg0,
    pg1,
    rg0,
    rg1,
    lsem,
    a2a_s,
    a2a_r,
    ag_s,
    ag_r,
    rs_s,
    rs_r,
    st_s,
    st_r,
):
    rows, width = tok.shape
    full = N_SLAB * width
    ff = win.shape[1]
    half = width // 2
    q = half // 4
    tile_w = width // 4
    half_rows = rows // 2
    slots = n_exp * ROWS
    me = lax.axis_index("expert")
    slab = lax.axis_index("slab")
    hi, core = slab // 2, slab % 2
    partner = hi * 2 + (1 - core)
    far = (1 - hi) * 2 + core
    far_partner = (1 - hi) * 2 + (1 - core)

    cp_tok = pltpu.make_async_copy(tok_hbm, tok, lsem.at[0])
    cp_dy = pltpu.make_async_copy(dy_hbm, gdy, lsem.at[1])
    cp_win = pltpu.make_async_copy(win_hbm, win, lsem.at[2])
    cp_wout = pltpu.make_async_copy(wout_hbm, wout, lsem.at[3])
    cp_tok.start()
    cp_dy.start()

    bar = pltpu.get_barrier_semaphore()

    @pl.loop(1, n_exp)
    def _(k):
        pl.semaphore_signal(
            bar, inc=1, device_id={"expert": lax.rem(me + k, n_exp)}, device_id_type=MESH
        )

    for peer in (partner, far, far_partner):
        pl.semaphore_signal(bar, inc=1, device_id={"slab": peer}, device_id_type=MESH)
    cp_win.start()
    cp_wout.start()

    pos = pos_ref[...]
    tgt = lax.div(pos, rows)
    row = pos - tgt * rows
    hit = iota((n_exp, rows), 0) == tgt
    before = dot(onehot(hit), onehot(iota((rows, rows), 0) < iota((rows, rows), 1)))
    rank = jnp.sum(jnp.where(hit, before, 0.0), axis=0, keepdims=True).astype(jnp.int32)
    third = lax.shift_right_logical(rank * 11, 5)
    rem3 = rank - 3 * third
    slot = [tgt * ROWS + rank]
    for j in range(3):
        slot.append(jnp.where(rem3 == j, tgt * ROWS + 12 + third, -1))
    for k in range(4):
        pick[k] = onehot(iota((slots, rows), 0) == slot[k])

    row_one = jnp.broadcast_to((row + 1).astype(F32), (128, rows))
    meta = None
    for k in range(4):
        marks = jnp.where(iota((128, rows), 0) // 32 == k, row_one, 0.0).astype(BF16)
        term = dot_t(pick[k], marks)
        meta = term if meta is None else meta + term
    px0[:, pl.ds(3 * q, 128)] = meta.astype(BF16)

    mine = pl.ds(pl.multiple_of(me * ROWS, ROWS), ROWS)

    def pack(into, keep, take, source, c):
        last = source[:, pl.ds(c * half + 3 * q, q)]
        for j in range(3):
            cs = pl.ds(j * q, q)
            value = dot(take[0], source[:, pl.ds(c * half + j * q, q)]) + dot(take[1 + j], last)
            into[:, cs] = value.astype(BF16)
        keep[mine, :] = into[mine, :]

    def unpack(into, lead, take, source, c):
        into[lead + (slice(None), pl.ds(c * half, 3 * q))] = dot(
            take[0], source[:, pl.ds(0, 3 * q)]
        ).astype(BF16)
        value = dot(take[1], source[:, pl.ds(0, q)])
        value += dot(take[2], source[:, pl.ds(q, q)])
        value += dot(take[3], source[:, pl.ds(2 * q, q)])
        into[lead + (slice(None), pl.ds(c * half + 3 * q, q))] = value.astype(BF16)

    def send_all(source, target, idx):
        @pl.loop(1, n_exp)
        def _(k):
            d = lax.rem(me + k, n_exp)
            pltpu.make_async_remote_copy(
                src_ref=source.at[pl.ds(pl.multiple_of(d * ROWS, ROWS), ROWS)],
                dst_ref=target.at[mine],
                send_sem=a2a_s.at[idx],
                recv_sem=a2a_r.at[idx],
                device_id={"expert": d},
                device_id_type=MESH,
            ).start()

    def wait_bytes(ref, sem):
        part = ref.at[pl.ds(0, (n_exp - 1) * ROWS)]
        pltpu.make_async_copy(part, part, sem).wait()

    cp_tok.wait()
    pack(px0, rx0, pick, tok, 0)
    pl.semaphore_wait(bar, n_exp - 1 + 3)
    send_all(px0, rx0, 0)
    pack(px1, rx1, pick, tok, 1)
    send_all(px1, rx1, 1)
    cp_dy.wait()
    pack(pd0, rd0, pick, gdy, 0)
    pack(pd1, rd1, pick, gdy, 1)

    for k in range(4):
        turned = jnp.transpose(jnp.broadcast_to(slot[k].astype(F32), (128, rows)))[:, 0:1]
        pick_t[k] = onehot(iota((rows, slots), 1).astype(F32) == turned)
    cp_win.wait()
    gain_rows = jnp.broadcast_to(gain_ref[...], (16, full))

    @pl.loop(0, ff // 256)
    def _(n):
        cs = pl.ds(pl.multiple_of(n * 256, 256), 256)
        usum[:, cs] = dot(gain_rows, win[:, cs])[0:8]

    def gather_copy(buf, idx, rs, c, source, kind, to):
        block = buf.at[source, rs, pl.ds(c * half, half)]
        return pltpu.make_async_remote_copy(
            src_ref=block,
            dst_ref=block,
            send_sem=ag_s.at[idx * 3 + kind],
            recv_sem=ag_r.at[idx * 3 + kind],
            device_id={"slab": to},
            device_id_type=MESH,
        )

    every = pl.ds(0, rows)

    def x_copy(c, source, kind, to):
        return gather_copy(xf, c, every, c, source, kind, to)

    def d_copy(h, c, source, kind, to):
        return gather_copy(
            df, 2 + 2 * h + c, pl.ds(h * half_rows, half_rows), c, source, kind, to
        )

    def x_dense(recv, c):
        unpack(xf, (slab,), comp, recv, c)
        x_copy(c, slab, 0, far).start()
        x_copy(c, slab, 1, partner).start()

    def d_start(h, c):
        d_copy(h, c, slab, 0, far).start()
        d_copy(h, c, slab, 1, partner).start()

    wait_bytes(rx0, a2a_r.at[0])
    marks_in = rx0[:, pl.ds(3 * q, 128)].astype(F32)
    marks_t = jnp.transpose(marks_in)
    for k in range(4):
        comp[k] = onehot((iota((rows, slots), 0) + 1).astype(F32) == marks_t[32 * k : 32 * k + 1])
    x_dense(rx0, 0)
    send_all(pd0, rd0, 2)
    wait_bytes(rx1, a2a_r.at[1])
    x_dense(rx1, 1)
    send_all(pd1, rd1, 3)
    for k in range(4):
        comp_t[k] = onehot(
            (iota((slots, rows), 1) + 1).astype(F32) == marks_in[:, 32 * k : 32 * k + 1]
        )
    x_copy(0, far, 0, far).wait_recv()
    x_copy(0, far, 2, partner).start()
    wait_bytes(rd0, a2a_r.at[2])
    unpack(df, (slab,), comp, rd0, 0)
    d_start(0, 0)
    x_copy(1, far, 0, far).wait_recv()
    x_copy(1, far, 2, partner).start()
    wait_bytes(rd1, a2a_r.at[3])
    unpack(df, (slab,), comp, rd1, 1)
    d_start(0, 1)
    d_start(1, 0)
    d_start(1, 1)
    for c in range(2):
        x_copy(c, partner, 1, partner).wait_recv()
    for c in range(2):
        x_copy(c, far_partner, 2, partner).wait_recv()

    step = 16

    @pl.loop(0, rows // step, unroll=2)
    def _(i):
        rs = pl.ds(pl.multiple_of(i * step, step), step)
        xs = [xf[b, rs, :].astype(F32) for b in range(N_SLAB)]
        total = None
        logit = None
        for b in range(N_SLAB):
            c_b = cent_ref[:, pl.ds(b * width, width)].astype(F32)
            t_b = jnp.sum(xs[b], axis=1, keepdims=True)
            l_b = jnp.sum(xs[b] * c_b, axis=1, keepdims=True)
            total = t_b if total is None else total + t_b
            logit = l_b if logit is None else logit + l_b
        mean = total * (1.0 / full)
        spread = None
        for b in range(N_SLAB):
            xs[b] = xs[b] - mean
            v_b = jnp.sum(xs[b] * xs[b], axis=1, keepdims=True)
            spread = v_b if spread is None else spread + v_b
        inv = lax.rsqrt(spread * (1.0 / full) + 1e-05)
        for b in range(N_SLAB):
            g_b = gain_ref[:, pl.ds(b * width, width)].astype(F32)
            nx[b, rs, :] = (xs[b] * inv * g_b).astype(BF16)
        gate = 1.0 / (1.0 + jnp.exp(-logit))
        cols[0, rs, :] = jnp.broadcast_to(mean, (step, 128))
        cols[1, rs, :] = jnp.broadcast_to(inv, (step, 128))
        cols[2, rs, :] = jnp.broadcast_to(gate, (step, 128))
    for n in range(ff // 256):
        cs = pl.ds(n * 256, 256)
        acc = dot(nx[0], win[pl.ds(0, width), cs])
        for b in range(1, N_SLAB):
            acc += dot(nx[b], win[pl.ds(b * width, width), cs])
        pre[:, cs] = acc

    @pl.loop(0, rows // step, unroll=2)
    def _(i):
        rs = pl.ds(pl.multiple_of(i * step, step), step)
        p = pre[rs, :]
        gate = cols[2, rs, 0:1]
        sq = p * p
        tangent = jnp.tanh(ROOT * (p + 0.044715 * p * sq))
        mid = 0.5 * (1.0 + tangent)
        act[rs, :] = p * mid
        slp[rs, :] = gate * (
            mid + 0.5 * p * (1.0 - tangent * tangent) * ROOT * (1.0 + 3.0 * 0.044715 * sq)
        )

    cp_wout.wait()

    def back_from(h, sources, first):
        hs = pl.ds(h * half_rows, half_rows)

        for n in range(ff // 256):
            rs = pl.ds(n * 256, 256)
            value = None
            for b in sources:
                base = pl.multiple_of(b * width, width)
                term = dot_t(df[b, hs, :], wout[rs, pl.ds(base, width)])
                value = term if value is None else value + term
            if first:
                bk[hs, rs] = value
            else:
                bk[hs, rs] += value

    def grad_tile(b, tile, rs):
        base = pl.multiple_of(b * width + tile * tile_w, tile_w)
        return dot_t(delta[rs, :], win[pl.ds(base, tile_w), :])

    def reduce_copy(kind, n, src, dst, to):
        return pltpu.make_async_remote_copy(
            src_ref=src.at[n],
            dst_ref=dst.at[n],
            send_sem=rs_s.at[kind * 8 + n],
            recv_sem=rs_r.at[kind * 8 + n],
            device_id={"slab": to},
            device_id_type=MESH,
        )

    def part_copy(n):
        return reduce_copy(0, n, part_send, part_recv, partner)

    def far_copy(n):
        return reduce_copy(1, n, far_send, far_recv, far)

    def mine_copy(n):
        return reduce_copy(2, n, mine_send, mine_recv, partner)

    def forward(h):
        for c in range(2):
            d_copy(h, c, far, 0, far).wait_recv()
            d_copy(h, c, far, 2, partner).start()

    def arrived(h, source, kind):
        for c in range(2):
            d_copy(h, c, source, kind, partner).wait_recv()

    def delta_of(h):
        @pl.loop(0, half_rows // step, unroll=4)
        def _(i):
            rs = pl.ds(pl.multiple_of(h * half_rows + i * step, step), step)
            b = bk[rs, :]
            d = (b * slp[rs, :]).astype(BF16)
            delta[rs, :] = d
            d = d.astype(F32)
            g_sum = jnp.sum(act[rs, :] * b, axis=1, keepdims=True)
            one = jnp.sum(d * usum[0:1, :], axis=1, keepdims=True)
            two = jnp.sum(d * pre[rs, :], axis=1, keepdims=True)
            lane = iota((step, 128), 1)
            cols[3, rs, :] = jnp.where(lane == 0, g_sum, jnp.where(lane == 1, one, two))

    def parts(h):
        hs = pl.ds(h * half_rows, half_rows)
        for tile in range(4):
            part_send[h * 4 + tile] = grad_tile(far_partner, tile, hs).astype(BF16)
            part_copy(h * 4 + tile).start()

    def fars(h):
        hs = pl.ds(h * half_rows, half_rows)
        for tile in range(4):
            value = grad_tile(far, tile, hs)
            part_copy(h * 4 + tile).wait_recv()
            far_send[h * 4 + tile] = (value + part_recv[h * 4 + tile].astype(F32)).astype(BF16)
            far_copy(h * 4 + tile).start()

    def stat_copy(n, to):
        return pltpu.make_async_remote_copy(
            src_ref=stat.at[0],
            dst_ref=stat.at[n],
            send_sem=st_s.at[n],
            recv_sem=st_r.at[n],
            device_id={"slab": to},
            device_id_type=MESH,
        )

    arrived(0, partner, 1)
    back_from(0, (slab, partner), True)
    forward(0)
    back_from(0, (far,), False)
    arrived(0, far_partner, 2)
    back_from(0, (far_partner,), False)
    delta_of(0)
    parts(0)
    arrived(1, partner, 1)
    forward(1)
    back_from(1, (slab, partner), True)
    fars(0)
    back_from(1, (far,), False)
    arrived(1, far_partner, 2)
    back_from(1, (far_partner,), False)
    delta_of(1)
    parts(1)
    stat[0] = jnp.transpose(cols[3])[0:8]
    peers = ((1, partner), (2, far), (3, far_partner))
    for n, to in peers:
        stat_copy(n, to).start()
    fars(1)
    for tile in range(4):
        mine_send[tile] = grad_tile(partner, tile, every).astype(BF16)
        mine_copy(tile).start()
    for tile in range(4):
        own[tile] = grad_tile(slab, tile, every)
    for n, to in peers:
        stat_copy(n, to).wait_recv()
    sums = stat[0] + stat[1] + stat[2] + stat[3]
    sums = jnp.transpose(jnp.concatenate([sums] * 16, axis=0))
    gate = cols[2, :, 0:1]
    gate_grad = sums[:, 0:1] * gate * (1.0 - gate)
    mean_one = sums[:, 1:2] * (1.0 / full)
    mean_two = sums[:, 2:3] * (1.0 / full)
    mean = cols[0, :, 0:1]
    inv = cols[1, :, 0:1]

    for tile in range(4):
        cs = pl.ds(tile * tile_w, tile_w)
        x = xf[slab, :, cs].astype(F32)
        cgrad_ref[:, cs] = jnp.sum(x * gate_grad, axis=0, keepdims=True)
        mine_copy(tile).wait_recv()
        own[tile] += mine_recv[tile].astype(F32)
    for tile in range(4):
        cs = pl.ds(tile * tile_w, tile_w)
        glob = pl.ds(pl.multiple_of(slab * width + tile * tile_w, tile_w), tile_w)
        gain_part = gain_ref[:, glob].astype(F32)
        cent_part = cent_ref[:, glob].astype(F32)
        for h in range(2):
            lo, up = h * half_rows, (h + 1) * half_rows
            hs = pl.ds(lo, half_rows)
            x = xf[slab, hs, cs].astype(F32)
            far_copy(h * 4 + tile).wait_recv()
            total = own[tile, hs, :] + far_recv[h * 4 + tile].astype(F32)
            scaled = total * gain_part
            hat = (x - mean[lo:up]) * inv[lo:up]
            value = inv[lo:up] * (scaled - mean_one[lo:up] - hat * mean_two[lo:up])
            value = value + gate_grad[lo:up] * cent_part
            yy[hs, cs] = value.astype(BF16)
        if tile == 1:
            pack(pg0, rg0, comp_t, yy, 0)
            send_all(pg0, rg0, 4)
    pack(pg1, rg1, comp_t, yy, 1)
    send_all(pg1, rg1, 5)
    wait_bytes(rg0, a2a_r.at[4])
    unpack(out_ref, (), pick_t, rg0, 0)
    wait_bytes(rg1, a2a_r.at[5])
    unpack(out_ref, (), pick_t, rg1, 1)

    for idx, buf in enumerate((px0, px1, pd0, pd1, pg0, pg1)):
        wait_bytes(buf, a2a_s.at[idx])
    for c in range(2):
        x_copy(c, slab, 0, far).wait_send()
        x_copy(c, slab, 1, partner).wait_send()
        x_copy(c, far, 2, partner).wait_send()
        for h in range(2):
            d_copy(h, c, slab, 0, far).wait_send()
            d_copy(h, c, slab, 1, partner).wait_send()
            d_copy(h, c, far, 2, partner).wait_send()
    for n in range(8):
        part_copy(n).wait_send()
        far_copy(n).wait_send()
    for n in range(4):
        mine_copy(n).wait_send()
    for n, to in peers:
        stat_copy(n, to).wait_send()


def hand_on(out_in, cgrad_in, out_ref, cgrad_ref):
    out_ref[...] = out_in[...]
    cgrad_ref[...] = cgrad_in[...]


def per_device(tokens, grad_out, position, centroid, gain, w_in, w_out):
    n_exp = lax.axis_size("expert")
    rows, width = tokens.shape
    full = centroid.shape[1]
    ff = w_in.shape[2]
    slots = n_exp * ROWS
    packed = 3 * width // 8
    vmem = pl.BlockSpec(memory_space=pltpu.VMEM)
    hbm = pl.BlockSpec(memory_space=pl.ANY)
    buf = pltpu.VMEM
    dma = pltpu.SemaphoreType.DMA
    shapes = (
        jax.ShapeDtypeStruct((rows, width), BF16),
        jax.ShapeDtypeStruct((1, width), F32),
    )
    out, cgrad = pl.pallas_call(
        functools.partial(kernel, n_exp),
        out_shape=shapes,
        in_specs=[vmem, vmem, vmem, hbm, hbm, hbm, hbm],
        out_specs=(vmem, vmem),
        scratch_shapes=[
            buf((rows, width), BF16),
            buf((rows, width), BF16),
            buf((full, ff), BF16),
            buf((ff, full), BF16),
            buf((4, slots, rows), BF16),
            buf((4, rows, slots), BF16),
            buf((slots, packed + 128), BF16),
            buf((slots, packed), BF16),
            buf((slots, packed), BF16),
            buf((slots, packed), BF16),
            buf((slots, packed + 128), BF16),
            buf((slots, packed), BF16),
            buf((slots, packed), BF16),
            buf((slots, packed), BF16),
            buf((4, rows, slots), BF16),
            buf((4, slots, rows), BF16),
            buf((N_SLAB, rows, width), BF16),
            buf((N_SLAB, rows, width), BF16),
            buf((N_SLAB, rows, width), BF16),
            buf((rows, ff), F32),
            buf((rows, ff), F32),
            buf((rows, ff), F32),
            buf((rows, ff), F32),
            buf((rows, ff), BF16),
            buf((8, ff), F32),
            buf((4, rows, 128), F32),
            buf((4, 8, rows), F32),
            buf((8, rows // 2, width // 4), BF16),
            buf((8, rows // 2, width // 4), BF16),
            buf((8, rows // 2, width // 4), BF16),
            buf((8, rows // 2, width // 4), BF16),
            buf((4, rows, width // 4), BF16),
            buf((4, rows, width // 4), BF16),
            buf((4, rows, width // 4), F32),
            buf((rows, width), BF16),
            buf((slots, packed), BF16),
            buf((slots, packed), BF16),
            buf((slots, packed), BF16),
            buf((slots, packed), BF16),
            dma((4,)),
            dma((6,)),
            dma((6,)),
            dma((18,)),
            dma((18,)),
            dma((20,)),
            dma((20,)),
            dma((4,)),
            dma((4,)),
        ],
        compiler_params=pltpu.CompilerParams(
            collective_id=0, has_side_effects=True, vmem_limit_bytes=56 * 2**20
        ),
        cost_estimate=pl.CostEstimate(
            flops=3 * 2 * rows * full * ff, bytes_accessed=4 * full * ff, transcendentals=rows * ff
        ),
    )(position.reshape(1, rows), centroid, gain, tokens, grad_out, w_in[0], w_out[0])
    return pl.pallas_call(
        hand_on,
        out_shape=shapes,
        in_specs=[vmem, vmem],
        out_specs=(vmem, vmem),
    )(out, cgrad)


def solution(mesh):
    placed = (
        P("expert", "slab"),
        P("expert", "slab"),
        P("expert"),
        P("expert", None),
        P("expert", None),
        P("expert", None, "slab"),
        P("expert", "slab", None),
    )
    return jax.shard_map(
        per_device,
        mesh=mesh,
        in_specs=placed,
        out_specs=(P("expert", "slab"), P("expert", "slab")),
        check_vma=False,
    )
```
